32 devices in a mesh: users: 8 (over z, y), items: 4 (over x, core).
Axes of the slice: x: 2, y: 2, z: 4, core: 2. Of those that a mesh axis runs over, the one named last changes fastest.
Arguments:
- user_factor: bfloat16 [16384, 256], P('users'), may hold values from -2.390625 to 2.390625
- hot_factor: bfloat16 [512, 256], replicated, may hold values from -2.390625 to 2.390625
- cold_factor: bfloat16 [8192, 256], P(('users', 'items')), may hold values from -2.390625 to 2.390625
- hour_factor: bfloat16 [168, 256], replicated, may hold values from -2.390625 to 2.390625
- block_user: int32 [32, 512], P(('users', 'items')), may hold values from 0 to 2047
- block_slot: int32 [32, 512], P(('users', 'items')), may hold values from 0 to 47
- block_hour: int32 [32, 512], P(('users', 'items')), may hold values from 0 to 20
- block_count: int32 [32], P(('users', 'items')), may hold values from 128 to 512, as said below
- need_rows: int32 [32, 8, 2], P(('users', 'items')), may hold values from 0 to 15
- observed: bfloat16 [32, 512, 128], P(('users', 'items')), may hold values from 0 to 1, as said below
Outputs:
- user_grad: float32 [16384, 256], P(('users', 'items'))
- cold_grad: float32 [8192, 256], P(('users', 'items'))
- hot_grad: float32 [512, 256], P(('users', 'items'))
- hour_grad: float32 [168, 256], replicated
The draws below stay inside these ranges and needn't reach their ends.
Inputs may be any that keep to these rules, and one draw needn't show every extreme that they name: `block_count`: some device has all 512 slots live. `observed`: every entry is 0 or 1.
All inputs are finite; a program needn't handle non-finite values.
Results may differ from the reference program's by a relative error of at most 0.0029.
Values may be sent and summed in bfloat16 or wider, within the bound.
No kernel may reach another device: no remote copies, remote signals or barrier semaphores. Data moves between devices by JAX's collectives and lax.ppermute only.
A program may use at most 128 MiB of HBM per device.

```python
import jax
import jax.numpy as jnp
from jax import lax

RANK = 256
HOURS = 168
IB = 16
HB = 8
HOT = 512
USER_DEV = 2048
ITEM_DEV = 256
REQ = 2
NBLK = 512
HOUR_BLOCKS = 21
USERS = 16384
ITEMS_COLD = 8192
SLOTS = 48
N_USERS = 8
N_ITEMS = 4


def draw_block_count(key, part):
    device_count = N_USERS * N_ITEMS
    counts = jax.random.randint(key, (device_count,), NBLK // 4, NBLK + 1)
    chosen = jax.random.randint(jax.random.fold_in(key, 7), (), 0, device_count)
    return counts.at[chosen].set(NBLK).astype(jnp.int32)


def draw_observed(key, part):
    device_count = N_USERS * N_ITEMS
    values = jax.random.bernoulli(key, 0.5, (device_count, NBLK, IB * HB)).astype(jnp.float32)
    return values.astype(jnp.bfloat16)


def touch_ends(values, stream_key, smallest, largest):
    extent = values.shape
    index_at = [jax.random.randint(jax.random.fold_in(stream_key, axis), (), 0, extent[axis]) for axis in range(len(extent))]
    values = values.at[tuple(index_at)].set(smallest)
    longest = extent.index(max(extent))
    index_at[longest] = (index_at[longest] + 1) % extent[longest]
    return values.at[tuple(index_at)].set(largest)


def block_scale(rng, extent, split, smallest, largest):
    def one(position, shards_of):
        steps = jax.random.uniform(jax.random.fold_in(jax.random.fold_in(rng, 6), position), (shards_of,), jnp.float32, smallest / len(split), largest / len(split))
        return jnp.repeat(jnp.exp(steps), extent[position] // shards_of).reshape((-1,) + (1,) * (len(extent) - position - 1))

    gain = one(*split[0])
    for cut in split[1:]:
        gain = gain * one(*cut)
    return gain


def gaussian(stream_key, dims, deviation, reach, shards=(), held_as=jnp.bfloat16):
    values = jax.random.normal(stream_key, dims, jnp.float32) * deviation
    if len(shards) > 0:
        values = block_scale(stream_key, dims, shards, -0.22, 0.18) * values
    return jnp.clip(values, min=-reach, max=reach).astype(held_as)


def setup_inputs(seed: int = 0) -> dict:
    streams_of = jax.random.split(jax.random.key(seed), 11)
    user_factor = gaussian(streams_of[0], (USERS, RANK), 0.4, 2.390625, ((0, 8),))
    hot_factor = gaussian(streams_of[1], (HOT, RANK), 0.4, 2.390625)
    cold_factor = gaussian(streams_of[2], (ITEMS_COLD, RANK), 0.4, 2.390625, ((0, 32),))
    hour_factor = gaussian(streams_of[3], (HOURS, RANK), 0.4, 2.390625)
    block_user = touch_ends(jax.random.randint(streams_of[4], (N_USERS * N_ITEMS, NBLK), 0, USER_DEV), jax.random.fold_in(streams_of[4], 1), 0, USER_DEV - 1).astype(jnp.int32)
    block_slot = touch_ends(jax.random.randint(streams_of[5], (N_USERS * N_ITEMS, NBLK), 0, SLOTS), jax.random.fold_in(streams_of[5], 1), 0, SLOTS - 1).astype(jnp.int32)
    block_hour = touch_ends(jax.random.randint(streams_of[6], (N_USERS * N_ITEMS, NBLK), 0, HOUR_BLOCKS), jax.random.fold_in(streams_of[6], 1), 0, HOUR_BLOCKS - 1).astype(jnp.int32)
    block_count = draw_block_count(jax.random.fold_in(streams_of[10], 71), 0)
    need_rows = touch_ends(jax.random.randint(streams_of[8], (N_USERS * N_ITEMS, N_USERS, REQ), 0, ITEM_DEV // IB), jax.random.fold_in(streams_of[8], 1), 0, (ITEM_DEV // IB) - 1).astype(jnp.int32)
    observed = draw_observed(jax.random.fold_in(streams_of[10], 71), 0)
    return {"user_factor": user_factor, "hot_factor": hot_factor, "cold_factor": cold_factor, "hour_factor": hour_factor, "block_user": block_user, "block_slot": block_slot, "block_hour": block_hour, "block_count": block_count, "need_rows": need_rows, "observed": observed}


def reference(user_factor, hot_factor, cold_factor, hour_factor, block_user, block_slot, block_hour, block_count, need_rows, observed):
    device_count = N_USERS * N_ITEMS
    device_ids = jnp.arange(device_count, dtype=jnp.int32)
    slab_index = device_ids // N_ITEMS
    column_index = device_ids % N_ITEMS
    hot_blocks = HOT // IB
    global_user = slab_index[:, None] * USER_DEV + block_user
    cold_slot = jnp.maximum(block_slot - hot_blocks, 0).astype(jnp.int32)
    peer_index = cold_slot // REQ
    flat_need = need_rows.reshape(device_count, N_USERS * REQ)
    picked_block = jnp.take_along_axis(flat_need, cold_slot, axis=1)
    cold_row = (peer_index * N_ITEMS + column_index[:, None]) * ITEM_DEV + picked_block * IB
    first_row = jnp.where(block_slot < hot_blocks, block_slot * IB, HOT + cold_row).astype(jnp.int32)
    live_mask = jnp.arange(NBLK, dtype=jnp.int32)[None, :] < block_count[:, None]
    group_len = min(NBLK, 512)
    total = device_count * NBLK
    groups = total // group_len
    item_table = jnp.concatenate([hot_factor, cold_factor], axis=0)
    offsets = jnp.arange(IB, dtype=jnp.int32)
    hour_offsets = jnp.arange(HB, dtype=jnp.int32)
    data = (global_user.reshape(groups, group_len), first_row.reshape(groups, group_len),
            block_hour.reshape(groups, group_len), live_mask.reshape(groups, group_len),
            observed.reshape(groups, group_len, IB, HB))

    def one_group(carry, group_data):
        grad_user, grad_item, grad_hour = carry
        users_idx, rows_idx, hours_idx, live, obs = group_data
        user_rows = user_factor[users_idx].astype(jnp.float32)
        item_idx = rows_idx[:, None] + offsets
        item_rows = item_table[item_idx].astype(jnp.float32)
        hour_rows = hour_factor[hours_idx[:, None] * HB + hour_offsets].astype(jnp.float32)
        user_item = (user_rows[:, None, :] * item_rows).astype(jnp.bfloat16)
        ui_wide = user_item.astype(jnp.float32)
        model = jnp.einsum('gar,gbr->gab', ui_wide, hour_rows)
        residual = jnp.where(live[:, None, None], jax.nn.sigmoid(model) - obs.astype(jnp.float32), 0.0).astype(jnp.bfloat16)
        res_wide = residual.astype(jnp.float32)
        weighted = jnp.einsum('gab,gbr->gar', res_wide, hour_rows)
        item_terms = weighted * user_rows[:, None, :]
        user_terms = jnp.sum(weighted * item_rows, axis=1)
        hour_terms = jnp.einsum('gab,gar->gbr', res_wide, ui_wide)
        grad_user = grad_user.at[users_idx].add(user_terms)
        grad_item = grad_item.at[item_idx.reshape(-1)].add(item_terms.reshape(-1, RANK))
        grad_hour = grad_hour.at[hours_idx].add(hour_terms.reshape(group_len, HB * RANK))
        return (grad_user, grad_item, grad_hour), None

    start = (jnp.zeros((USERS, RANK), jnp.float32), jnp.zeros((HOT + ITEMS_COLD, RANK), jnp.float32),
             jnp.zeros((HOUR_BLOCKS, HB * RANK), jnp.float32))
    (grad_user, grad_item, grad_hour), _ = lax.scan(one_group, start, data)
    return grad_user, grad_item[HOT:], grad_item[:HOT], grad_hour.reshape(HOURS, RANK)
```

```python
import functools

import jax
import jax.numpy as jnp
from jax import lax
from jax.experimental import pallas as pl
from jax.experimental.pallas import tpu as pltpu
from jax.sharding import PartitionSpec as P

IB = 16
HB = 8
HALF = 128
F32 = jnp.float32
BF16 = jnp.bfloat16


def bits_of(size):
    return size.bit_length() - 1


def flip(value, bits):
    out = jnp.zeros_like(value)
    for k in range(bits):
        out = out | (((value >> k) & 1) << (bits - 1 - k))
    return out


def hour_of(lane, split, hours):
    half = hours // 2
    inside = lane & (HALF - 1)
    hour = ((lane >> 7) ^ split) * half + inside
    return hour, inside < half


def kernel(
    sizes, ids, count, user, slot, hour, user_tab, hot, cold, hours_tab, observed,
    grad_user, grad_item, grad_hour,
    table, item_sums, user_rows, user_terms, obs, live_hour,
):
    peers, items, hot_slots, reqs, hours, permute_hot = sizes
    p, q = ids[0], ids[1]
    blocks = user.shape[1]
    users = user_tab.shape[0]
    slots = table.shape[1] // IB
    user_chunk = users // items
    parts = range(table.shape[0])

    for part in parts:
        lanes = slice(part * 128, part * 128 + 128)
        table[part, : hot.shape[0], :] = hot[:, lanes].astype(F32)
        table[part, hot.shape[0] :, :] = cold[:, lanes].astype(F32)

    def column(row):
        parts = [
            jnp.transpose(jnp.broadcast_to(row[:, k : k + 128], (128, 128))) for k in range(0, blocks, 128)
        ]
        return jnp.concatenate(parts, axis=0)

    def spread(col, lanes):
        return jnp.concatenate([col] * (-(-lanes // 128)), axis=1)[:, :lanes]

    user_row, slot_row = user[...], slot[...]
    place = lax.broadcasted_iota(jnp.int32, (1, blocks), 1)
    hour_row = jnp.where(place < count[0], hour[...], -1)
    user_col, slot_col = column(user_row), column(slot_row)
    hour_col = column(hour_row)

    step = 512
    acc = jnp.zeros((blocks, user_tab.shape[1]), F32)
    for k in range(0, users, step):
        lane = lax.broadcasted_iota(jnp.int32, (blocks, step), 1) + k
        hit = (spread(user_col, step) == lane).astype(F32).astype(BF16)
        acc += jnp.dot(hit, user_tab[k : k + step, :], preferred_element_type=F32)
    user_rows[...] = acc
    user_terms[...] = jnp.zeros_like(user_terms)
    grad_hour[...] = jnp.zeros_like(grad_hour)

    pick = (spread(slot_col, slots) == lax.broadcasted_iota(jnp.int32, (blocks, slots), 1)).astype(F32).astype(BF16)
    user_bits, all_bits = bits_of(peers), bits_of(peers * items)
    cold_slot = slot_row - hot_slots
    cold_pos = hot_slots + flip((cold_slot // reqs) ^ p, user_bits) * reqs + cold_slot % reqs
    hot_pos = flip(slot_row ^ (p * items + q), all_bits) if permute_hot else slot_row
    put_pos = jnp.where(slot_row < hot_slots, hot_pos, cold_pos)
    put = (put_pos == lax.broadcasted_iota(jnp.int32, (slots, blocks), 0)).astype(F32).astype(BF16)

    lane = lax.broadcasted_iota(jnp.int32, (blocks, 2 * HALF), 1)
    lane_hour, used = hour_of(lane, q & 1, hours)
    mask = used & ((lane_hour // HB) == spread(hour_col, 2 * HALF))
    live_hour[...] = mask.astype(F32)
    obs[...] = 0.5 - observed[...].astype(F32)
    lane_hour, used = hour_of(lax.broadcasted_iota(jnp.int32, (IB * HB, 2 * HALF), 1), q & 1, hours)
    cell = lax.broadcasted_iota(jnp.int32, (IB * HB, 2 * HALF), 0)
    tile = (used & ((cell & (HB - 1)) == (lane_hour & (HB - 1)))).astype(F32).astype(BF16)

    cell_item = lax.broadcasted_iota(jnp.int32, (blocks, IB * HB), 1) // HB
    hours_half = hours_tab[...] * jnp.asarray(0.5, BF16)

    def one(a):
        of_place = pl.ds(a, slots, stride=IB)
        choice = jnp.concatenate([table[part, of_place, :] for part in parts], axis=1).astype(BF16)
        rows = jnp.dot(pick, choice, preferred_element_type=F32)
        users_f = user_rows[...]
        user_item = (users_f * rows).astype(BF16)
        half_model = lax.dot_general(
            user_item, hours_half, (((1,), (1,)), ((), ())), preferred_element_type=F32
        )
        seen = jnp.dot(
            jnp.where(cell_item == a, obs[...], 0.0).astype(BF16), tile, preferred_element_type=F32
        )
        residual = ((0.5 * jnp.tanh(half_model) + seen) * live_hour[...]).astype(BF16)
        weighted = jnp.dot(residual, hours_tab[...], preferred_element_type=F32)
        grad_hour[...] += lax.dot_general(
            residual, user_item, (((0,), (0,)), ((), ())), preferred_element_type=F32
        )
        user_terms[...] += weighted * rows
        terms = weighted * users_f
        high = terms.astype(BF16)
        low = (terms - high.astype(F32)).astype(BF16)
        total = jnp.dot(put, high, preferred_element_type=F32) + jnp.dot(put, low, preferred_element_type=F32)
        for part in parts:
            item_sums[part, of_place, :] = total[:, part * 128 : part * 128 + 128]

    def loop(a, carry):
        one(a)
        return carry

    lax.fori_loop(0, IB, loop, 0)

    for part in parts:
        grad_item[:, part * 128 : part * 128 + 128] = item_sums[part]

    terms = user_terms[...]
    high = terms.astype(BF16)
    low = (terms - high.astype(F32)).astype(BF16)
    item_bits = bits_of(items)
    user_pos = flip((user_row // user_chunk) ^ q, item_bits) * user_chunk + user_row % user_chunk
    for k in range(0, users, step):
        hit = (user_pos == lax.broadcasted_iota(jnp.int32, (step, blocks), 0) + k).astype(F32).astype(BF16)
        grad_user[k : k + step, :] = jnp.dot(hit, high, preferred_element_type=F32) + jnp.dot(
            hit, low, preferred_element_type=F32
        )


def hop(values, axis, size, bit):
    return lax.ppermute(values, axis, [(i, i ^ (1 << bit)) for i in range(size)])


def halves(values):
    rows = values.shape[0] // 2
    return values[:rows], values[rows:]


def body(
    user_factor,
    hot_factor,
    cold_factor,
    hour_factor,
    block_user,
    block_slot,
    block_hour,
    block_count,
    need_rows,
    observed,
):
    rank_size = user_factor.shape[1]
    hours = hour_factor.shape[0]
    hot_rows = hot_factor.shape[0]
    shard_len = cold_factor.shape[0]
    peers, items = lax.axis_size("users"), lax.axis_size("items")
    p, q = lax.axis_index("users"), lax.axis_index("items")
    requests = need_rows[0]
    reqs = requests.shape[1]
    offsets = jnp.arange(IB, dtype=jnp.int32)
    asked = lax.all_to_all(requests, "users", split_axis=0, concat_axis=0, tiled=True)
    served_rows = (asked[:, :, None] * IB + offsets).reshape(-1)
    fetched = lax.all_to_all(
        cold_factor[served_rows].reshape(peers, reqs * IB, rank_size), "users", split_axis=0, concat_axis=0, tiled=True
    ).reshape(-1, rank_size)

    half = hours // 2
    pad = jnp.zeros((HALF - half, rank_size), BF16)
    low, high = halves(hour_factor)
    swap = (q & 1) == 1
    hour_table = jnp.concatenate([jnp.where(swap, high, low), pad, jnp.where(swap, low, high), pad], axis=0)

    blocks = block_user.shape[1]
    hot_slots = hot_rows // IB
    slots = hot_slots + peers * reqs
    permute_hot = hot_rows == IB * peers * items
    sizes = (peers, items, hot_slots, reqs, hours, permute_hot)
    vmem = pl.BlockSpec(memory_space=pltpu.VMEM)
    smem = pl.BlockSpec(memory_space=pltpu.SMEM)
    grad_user, grad_item, grad_hour = pl.pallas_call(
        functools.partial(kernel, sizes),
        out_shape=(
            jax.ShapeDtypeStruct(user_factor.shape, F32),
            jax.ShapeDtypeStruct((slots * IB, rank_size), F32),
            jax.ShapeDtypeStruct((2 * HALF, rank_size), F32),
        ),
        in_specs=[smem, smem] + [vmem] * 8,
        out_specs=(vmem, vmem, vmem),
        scratch_shapes=[
            pltpu.VMEM((rank_size // 128, slots * IB, 128), F32),
            pltpu.VMEM((rank_size // 128, slots * IB, 128), F32),
            pltpu.VMEM((blocks, rank_size), F32),
            pltpu.VMEM((blocks, rank_size), F32),
            pltpu.VMEM((blocks, IB * HB), F32),
            pltpu.VMEM((blocks, 2 * HALF), F32),
        ],
        compiler_params=pltpu.CompilerParams(vmem_limit_bytes=48 * 1024 * 1024),
        name="blocks",
    )(
        jnp.stack([p, q]).astype(jnp.int32),
        block_count,
        block_user,
        block_slot,
        block_hour,
        user_factor,
        hot_factor,
        fetched,
        hour_table,
        observed[0],
    )

    returned = grad_item[hot_rows:].astype(BF16).reshape(-1, reqs * IB, rank_size)
    hot = grad_item[:hot_rows]
    user = grad_user
    mine, other = halves(grad_hour)
    mine, other = mine[:half], other[:half]

    for bit in range(bits_of(items)):
        keep, send = halves(user)
        user = keep + hop(send.astype(BF16), "items", items, bit).astype(F32)
        if permute_hot:
            keep, send = halves(hot)
            hot = keep + hop(send.astype(BF16), "items", items, bit).astype(F32)
        if bit == 0:
            mine = mine + hop(other, "items", items, bit)
        else:
            mine = mine + hop(mine, "items", items, bit)
    for bit in range(bits_of(peers)):
        if permute_hot:
            keep, send = halves(hot)
            hot = keep + hop(send, "users", peers, bit)
        mine = mine + hop(mine, "users", peers, bit)
        size = returned.shape[0] // 2
        keep, send = returned[:size], returned[size:]
        returned = jnp.concatenate([keep, hop(send, "users", peers, bit)], axis=1)
    other = hop(mine, "items", items, 0)
    hour_grad = jnp.concatenate([jnp.where(swap, other, mine), jnp.where(swap, mine, other)], axis=0)
    if not permute_hot:
        hot = lax.psum_scatter(hot, ("users", "items"), scatter_dimension=0, tiled=True)

    returned = returned.reshape(peers, reqs, IB, rank_size)
    source = jnp.arange(peers, dtype=jnp.int32) ^ p
    wanted = asked[source].reshape(-1)
    shard_blocks = shard_len // IB
    hit = (jnp.arange(shard_blocks, dtype=jnp.int32)[:, None] == wanted[None, :]).astype(BF16)
    cold_grad = jnp.dot(hit, returned.reshape(peers * reqs, IB * rank_size), preferred_element_type=F32)
    return (user, cold_grad.reshape(shard_len, rank_size), hot, hour_grad)


def solution(mesh):
    in_specs = (
        P("users", None),
        P(),
        P(("users", "items"), None),
        P(),
        P(("users", "items"), None),
        P(("users", "items"), None),
        P(("users", "items"), None),
        P(("users", "items")),
        P(("users", "items"), None, None),
        P(("users", "items"), None, None),
    )
    out_specs = (
        P(("users", "items"), None),
        P(("users", "items"), None),
        P(("users", "items"), None),
        P(),
    )
    return jax.shard_map(body, mesh=mesh, in_specs=in_specs, out_specs=out_specs, check_vma=False)
```

```python
import collections
import functools

import jax
import jax.numpy as jnp
from jax import lax
from jax.experimental import pallas as pl
from jax.experimental.pallas import tpu as pltpu
from jax.sharding import PartitionSpec as P

IB = 16
HB = 8
HALF = 128
F32 = jnp.float32
BF16 = jnp.bfloat16

Sizes = collections.namedtuple(
    "Sizes",
    ("peers", "items", "hot_slots", "reqs", "hours", "permute_hot", "split_hot", "hot_blocks", "cold_blocks"),
)


def bits_of(size):
    return size.bit_length() - 1


def padded(rows):
    return -(-rows // 16) * 16


def flip(value, bits):
    out = jnp.zeros_like(value)
    for k in range(bits):
        out = out | (((value >> k) & 1) << (bits - 1 - k))
    return out


def hour_of(lane, split, hours):
    half = hours // 2
    inside = lane & (HALF - 1)
    hour = ((lane >> 7) ^ split) * half + inside
    return hour, inside < half


def one_hot(mask):
    return mask.astype(F32).astype(BF16)


def column(row):
    parts = [jnp.transpose(jnp.broadcast_to(row[:, k : k + 128], (128, 128))) for k in range(0, row.shape[1], 128)]
    return jnp.concatenate(parts, axis=0)


def spread(col, lanes):
    return jnp.concatenate([col] * (-(-lanes // 128)), axis=1)[:, :lanes]


def load_table(table, rows, at=0):
    for part in range(table.shape[0]):
        table[part, at : at + rows.shape[0], :] = rows[:, part * 128 : part * 128 + 128].astype(F32)


def chosen_blocks(sizes, hot, count, slot_row):
    place = lax.broadcasted_iota(jnp.int32, slot_row.shape, 1)
    of_kind = (slot_row < sizes.hot_slots) if hot else (slot_row >= sizes.hot_slots)
    chosen = (place < count) & of_kind
    return chosen, jnp.sum(chosen.astype(F32))


def prepare(sizes, hot, m, p, q, chosen, user, slot, hour, user_tab, observed, out):
    obs, live_hour, user_rows, pick, put, user_pos = out
    blocks = slot.shape[1]
    users = user_tab.shape[0]
    user_chunk = users // sizes.items

    kind = jnp.broadcast_to(chosen.astype(F32), (8, blocks)).astype(BF16)
    before = one_hot(
        lax.broadcasted_iota(jnp.int32, (blocks, blocks), 0) < lax.broadcasted_iota(jnp.int32, (blocks, blocks), 1)
    )
    rank = jnp.dot(kind, before, preferred_element_type=F32)[:1]
    rank = jnp.where(chosen, rank, -1.0).astype(jnp.int32)
    order = one_hot(rank == lax.broadcasted_iota(jnp.int32, (m, blocks), 0))
    user_in = user[...]
    rows = [user_in >> 4, user_in & 15, slot[...], hour[...] + 1]
    rows = jnp.concatenate([row.astype(F32) for row in rows] + [jnp.zeros((4, blocks), F32)], axis=0).astype(BF16)
    rows = lax.dot_general(rows, order, (((1,), (1,)), ((), ())), preferred_element_type=F32).astype(jnp.int32)
    user_row, slot_row, hour_row = rows[0:1] * 16 + rows[1:2], rows[2:3], rows[3:4] - 1
    obs[:m, :] = jnp.dot(order, 0.5 - observed[...], preferred_element_type=F32)

    user_col, hour_col = column(user_row), column(hour_row)
    step = 512
    total = jnp.zeros((m, user_tab.shape[1]), F32)
    for k in range(0, users, step):
        lane = lax.broadcasted_iota(jnp.int32, (m, step), 1) + k
        total += jnp.dot(one_hot(spread(user_col, step) == lane), user_tab[k : k + step, :], preferred_element_type=F32)
    user_rows[:m, :] = total

    slots = pick.shape[1]
    if hot:
        put_pos = flip(slot_row ^ (p * sizes.items + q), bits_of(sizes.peers * sizes.items)) if sizes.permute_hot else slot_row
    else:
        owner, request = (slot_row - sizes.hot_slots) // sizes.reqs, (slot_row - sizes.hot_slots) % sizes.reqs
        put_pos = (owner ^ p) * sizes.reqs + request
        slot_row = (owner ^ (p & ~1)) * sizes.reqs + request
    pick[:m, :] = one_hot(spread(column(slot_row), slots) == lax.broadcasted_iota(jnp.int32, (m, slots), 1))
    put[:, :m] = one_hot(put_pos == lax.broadcasted_iota(jnp.int32, (slots, m), 0))
    user_pos[:, :m] = flip((user_row // user_chunk) ^ q, bits_of(sizes.items)) * user_chunk + user_row % user_chunk

    lane = lax.broadcasted_iota(jnp.int32, (m, 2 * HALF), 1)
    lane_hour, used = hour_of(lane, q & 1, sizes.hours)
    live_hour[:m, :] = (used & ((lane_hour // HB) == spread(hour_col, 2 * HALF))).astype(F32)


def work(sizes, m, first, last, q, state, table, hours_tab, user_terms, item_sums, grad_hour, stack=4):
    obs, live_hour, user_rows, pick, put, _ = state
    slots = pick.shape[1]
    parts = range(table.shape[0])
    lane_hour, used = hour_of(lax.broadcasted_iota(jnp.int32, (IB * HB, 2 * HALF), 1), q & 1, sizes.hours)
    cell = lax.broadcasted_iota(jnp.int32, (IB * HB, 2 * HALF), 0)
    tile = one_hot(used & ((cell & (HB - 1)) == (lane_hour & (HB - 1))))
    cell_item = lax.broadcasted_iota(jnp.int32, (m, IB * HB), 1) // HB

    def one(group, carry):
        places = [group * stack + j for j in range(stack)]
        rows, cells = [], []
        for a in places:
            of_place = pl.ds(a, slots, stride=IB)
            choice = jnp.concatenate([table[part, of_place, :] for part in parts], axis=1).astype(BF16)
            rows.append(jnp.dot(pick[:m, :], choice, preferred_element_type=F32))
            cells.append(jnp.where(cell_item == a, obs[:m, :], 0.0).astype(BF16))
        users_f = user_rows[:m, :]
        user_item = jnp.concatenate([(users_f * row).astype(BF16) for row in rows], axis=0)
        half_model = lax.dot_general(
            user_item, hours_tab[...] * jnp.asarray(0.5, BF16), (((1,), (1,)), ((), ())), preferred_element_type=F32
        )
        seen = jnp.dot(jnp.concatenate(cells, axis=0), tile, preferred_element_type=F32)
        live = jnp.concatenate([live_hour[:m, :]] * stack, axis=0)
        residual = ((0.5 * jnp.tanh(half_model) + seen) * live).astype(BF16)
        weighted = jnp.dot(residual, hours_tab[...], preferred_element_type=F32)
        grad_hour[...] += lax.dot_general(
            residual, user_item, (((0,), (0,)), ((), ())), preferred_element_type=F32
        )
        into = put[:, :m]
        total = user_terms[:m, :]
        for j, a in enumerate(places):
            mine = weighted[j * m : j * m + m]
            total += mine * rows[j]
            terms = mine * users_f
            high = terms.astype(BF16)
            low = (terms - high.astype(F32)).astype(BF16)
            sums = jnp.dot(into, high, preferred_element_type=F32) + jnp.dot(into, low, preferred_element_type=F32)
            for part in parts:
                item_sums[part, pl.ds(a, slots, stride=IB), :] = sums[:, part * 128 : part * 128 + 128]
        user_terms[:m, :] = total
        return carry

    lax.fori_loop(first // stack, last // stack, one, 0)


def in_size(number, small, whole, run):
    pl.when(number <= small)(lambda: run(small))
    pl.when(number > small)(lambda: run(whole))


def serve(sizes, *refs):
    turns = sizes.peers // 2
    needs, (mine, theirs), outs, table = refs[: -turns - 3], refs[-turns - 3 : -turns - 1], refs[-turns - 1 : -1], refs[-1]
    p = lax.axis_index("users")
    rows = mine.shape[0]
    table[pl.ds(pl.multiple_of((p & 1) * rows, rows), rows), :] = mine[...]
    table[pl.ds(pl.multiple_of((1 - (p & 1)) * rows, rows), rows), :] = theirs[...]
    for m, out in enumerate(outs):
        for which in range(2):
            for r in range(sizes.reqs):
                owner = (p & ~1) + which
                block = needs[m][0, r, owner] if len(needs) == turns else needs[0][m, r * sizes.peers + owner]
                at = pl.multiple_of(which * rows + block * IB, IB)
                to = (which * sizes.reqs + r) * IB
                out[to : to + IB, :] = table[pl.ds(at, IB), :]


def start_copies(pairs, sems):
    copies = [pltpu.make_async_copy(source, target, sems.at[k]) for k, (source, target) in enumerate(pairs)]
    for copy in copies:
        copy.start()
    return copies


def first_kernel(
    sizes, count, user_in, slot_in, hour_in, user_tab_in, hot_in, hour_factor_in, observed_in,
    obs, live_hour, user_rows, pick, put, user_pos, user_terms, item_sums, grad_hour,
    table, hours_tab, user, slot, hour,
    user_tab, hot, hour_factor, observed, sems,
):
    state = (obs, live_hour, user_rows, pick, put, user_pos)
    p, q = lax.axis_index("users"), lax.axis_index("items")
    sources = (slot_in, user_in, hour_in, observed_in.at[0], user_tab_in, hour_factor_in, hot_in)
    copies = start_copies(zip(sources, (slot, user, hour, observed, user_tab, hour_factor, hot)), sems)
    user_terms[...] = jnp.zeros_like(user_terms)
    grad_hour[...] = jnp.zeros_like(grad_hour)
    for copy in copies[:3]:
        copy.wait()
    chosen, number = chosen_blocks(sizes, True, count[0], slot[...])
    for copy in copies[3:]:
        copy.wait()
    load_table(table, hot)
    row_hour, used = hour_of(lax.broadcasted_iota(jnp.int32, (2 * HALF, sizes.hours), 0), q & 1, sizes.hours)
    hit = one_hot(used & (row_hour == lax.broadcasted_iota(jnp.int32, (2 * HALF, sizes.hours), 1)))
    hours_tab[...] = jnp.dot(hit, hour_factor[...], preferred_element_type=F32).astype(BF16)

    def run(m):
        prepare(sizes, True, m, p, q, chosen, user, slot, hour, user_tab, observed, state)
        work(sizes, m, 0, IB // 2, q, state, table, hours_tab, user_terms, item_sums, grad_hour)

    in_size(number, sizes.hot_blocks, slot.shape[1], run)


def second_kernel(
    sizes, count, user_tab_in, observed_in,
    obs, live_hour, user_rows, pick, put, user_pos, user_terms_in, item_sums_in, grad_hour_in,
    table, hours_tab, user, slot, hour,
    obs_2, live_hour_2, user_rows_2, pick_2, put_2, user_pos_2, user_terms, item_sums, grad_hour,
    user_tab, observed, sems,
):
    state = (obs, live_hour, user_rows, pick, put, user_pos)
    state_2 = (obs_2, live_hour_2, user_rows_2, pick_2, put_2, user_pos_2)
    p, q = lax.axis_index("users"), lax.axis_index("items")
    copies = start_copies(zip((observed_in.at[0], user_tab_in), (observed, user_tab)), sems)
    user_terms[...] = user_terms_in[...]
    item_sums[...] = item_sums_in[...]
    grad_hour[...] = grad_hour_in[...]
    _, number = chosen_blocks(sizes, True, count[0], slot[...])

    def run(m):
        work(sizes, m, IB // 2, IB, q, state, table, hours_tab, user_terms, item_sums, grad_hour)

    in_size(number, sizes.hot_blocks, slot.shape[1], run)
    chosen, number = chosen_blocks(sizes, False, count[0], slot[...])
    for copy in copies:
        copy.wait()

    def make(m):
        prepare(sizes, False, m, p, q, chosen, user, slot, hour, user_tab, observed, state_2)

    in_size(number, sizes.cold_blocks, slot.shape[1], make)


def third_kernel(
    sizes, count, slot, hours_tab,
    obs, live_hour, user_rows, pick, put, user_pos, hot_sums, grad_hour_in,
    *refs,
):
    fetched, (send, keep, cold_send, user_terms, table, item_sums, grad_hour) = refs[:-7], refs[-7:]
    state = (obs, live_hour, user_rows, pick, put, user_pos)
    q = lax.axis_index("items")
    rows = fetched[0].shape[0]
    for m, block in enumerate(fetched):
        load_table(table, block, m * rows)
    user_terms[...] = jnp.zeros_like(user_terms)
    grad_hour[...] = grad_hour_in[...]
    _, number = chosen_blocks(sizes, False, count[0], slot[...])

    def run(m):
        work(sizes, m, 0, IB, q, state, table, hours_tab, user_terms, item_sums, grad_hour)

    in_size(number, sizes.cold_blocks, slot.shape[1], run)

    high_rows = padded(sizes.hours // 2)
    at = sizes.split_hot
    for part in range(table.shape[0]):
        lanes = slice(part * 128, part * 128 + 128)
        if at:
            keep[:at, lanes] = hot_sums[part, :at, :]
            send[:at, lanes] = hot_sums[part, at : 2 * at, :].astype(BF16)
        cold_send[:, lanes] = item_sums[part].astype(BF16)
    keep[at : at + high_rows, :] = grad_hour[:high_rows, :]
    other = grad_hour[HALF : HALF + high_rows, :]
    high = other.astype(BF16)
    send[at : at + high_rows, :] = high
    send[at + high_rows : at + 2 * high_rows, :] = (other - high.astype(F32)).astype(BF16)


def users_kernel(sizes, count, slot, pos, terms, pos_2, terms_2, send, keep, step=256):
    _, number = chosen_blocks(sizes, True, count[0], slot[...])
    _, number_2 = chosen_blocks(sizes, False, count[0], slot[...])

    def add(m, m_2):
        total = jnp.concatenate([terms[:m, :], terms_2[:m_2, :]], axis=0)
        high = total.astype(BF16)
        low = (total - high.astype(F32)).astype(BF16)
        row = jnp.concatenate([pos[:, :m], pos_2[:, :m_2]], axis=1)
        within = one_hot((row & (step - 1)) == lax.broadcasted_iota(jnp.int32, (step, m + m_2), 0))
        for k in range(0, 2 * keep.shape[0], step):
            hit = within * one_hot((row // step) == k // step)
            sums = jnp.dot(hit, high, preferred_element_type=F32) + jnp.dot(hit, low, preferred_element_type=F32)
            if k < keep.shape[0]:
                keep[k : k + step, :] = sums
            else:
                send[k - keep.shape[0] : k - keep.shape[0] + step, :] = sums.astype(BF16)

    def hot(m):
        in_size(number_2, sizes.cold_blocks, slot.shape[1], lambda m_2: add(m, m_2))

    in_size(number, sizes.hot_blocks, slot.shape[1], hot)


def finish(sizes, needs, returned, mine, other, hot, got, cold_grad, hot_grad, hour_grad):
    p, q = lax.axis_index("users"), lax.axis_index("items")
    hot_grad[...] = hot[...] + got[...].astype(F32)
    half = mine.shape[0]
    swap = (q & 1) == 1
    hour_grad[:half, :] = jnp.where(swap, other[...], mine[...])
    hour_grad[half:, :] = jnp.where(swap, mine[...], other[...])
    asked, rows = needs.shape[0], returned.shape[0]
    lane = lax.broadcasted_iota(jnp.int32, needs.shape, 1)
    mask = jnp.where(lane == p, needs[...], 0).astype(F32)
    wanted = jnp.broadcast_to(jnp.sum(mask, axis=1, keepdims=True), (asked, 128)).astype(BF16)
    number = lax.broadcasted_iota(jnp.int32, (asked, rows), 1) // IB
    source = flip(number // sizes.reqs, bits_of(sizes.peers)) * sizes.reqs + number % sizes.reqs
    place = one_hot(source == lax.broadcasted_iota(jnp.int32, (asked, rows), 0))
    block = lax.dot_general(wanted, place, (((0,), (0,)), ((), ())), preferred_element_type=F32)[:1].astype(jnp.int32)
    size = (cold_grad.shape[0], rows)
    row, column = lax.broadcasted_iota(jnp.int32, size, 0), lax.broadcasted_iota(jnp.int32, size, 1)
    hit = one_hot((row // IB == block) & (row % IB == column % IB))
    cold_grad[...] = jnp.dot(hit, returned[...], preferred_element_type=F32)


def hop(values, axis, size, bit):
    return lax.ppermute(values, axis, [(i, i ^ (1 << bit)) for i in range(size)])


def turn(values, axis, size, change):
    return lax.ppermute(values, axis, [(i, i ^ change) for i in range(size)])


def halves(values):
    rows = values.shape[0] // 2
    return values[:rows], values[rows:]


def body(
    user_factor,
    hot_factor,
    cold_factor,
    hour_factor,
    block_user,
    block_slot,
    block_hour,
    block_count,
    need_rows,
    observed,
):
    rank_size = user_factor.shape[1]
    hours = hour_factor.shape[0]
    hot_rows = hot_factor.shape[0]
    shard_len = cold_factor.shape[0]
    peers, items = lax.axis_size("users"), lax.axis_size("items")
    reqs = need_rows.shape[2]
    half = hours // 2
    blocks = block_user.shape[1]
    users = user_factor.shape[0]
    hot_slots, cold_slots = hot_rows // IB, peers * reqs
    permute_hot = hot_rows == IB * peers * items
    high_rows = padded(half)
    split_hot = hot_rows // 2 if permute_hot else 0
    sizes = Sizes(
        peers, items, hot_slots, reqs, hours, permute_hot, split_hot, blocks // 4 * 3, blocks // 2
    )
    vmem = pl.BlockSpec(memory_space=pltpu.VMEM)
    smem = pl.BlockSpec(memory_space=pltpu.SMEM)
    hbm = pl.BlockSpec(memory_space=pltpu.HBM)

    def shape(*dims, dtype=F32):
        return jax.ShapeDtypeStruct(dims, dtype)

    def state_of(slots):
        return (
            shape(blocks, IB * HB),
            shape(blocks, 2 * HALF),
            shape(blocks, rank_size),
            shape(blocks, slots, dtype=BF16),
            shape(slots, blocks, dtype=BF16),
            shape(1, blocks, dtype=jnp.int32),
        )

    def table_of(slots):
        return (rank_size // 128, slots * IB, 128)

    def call(function, scalar, far, near, out_shape, scratch, flops):
        return pl.pallas_call(
            functools.partial(function, sizes),
            out_shape=out_shape,
            in_specs=[smem] * len(scalar) + [hbm] * len(far) + [vmem] * len(near),
            out_specs=(vmem,) * len(out_shape),
            scratch_shapes=scratch,
            compiler_params=pltpu.CompilerParams(vmem_limit_bytes=24 * 1024 * 1024),
            cost_estimate=pl.CostEstimate(flops=flops, bytes_accessed=4 << 20, transcendentals=0),
            name=function.__name__,
        )(*scalar, *[pltpu.with_memory_space_constraint(value, pltpu.HBM) for value in far], *near)

    turns = peers // 2
    theirs = hop(cold_factor, "users", peers, 0)
    need = jnp.transpose(need_rows, (0, 2, 1))
    needs = [need] + [turn(need, "users", peers, 2 * m) for m in range(1, turns)]

    def room(*dims, dtype=F32):
        return pltpu.VMEM(dims, dtype)

    row = shape(1, blocks, dtype=jnp.int32)
    sums = (shape(*table_of(hot_slots)), shape(2 * HALF, rank_size))
    users_room = room(*user_factor.shape, dtype=BF16)
    observed_room = room(*observed.shape[1:], dtype=BF16)
    hot_state = call(
        first_kernel,
        (block_count,),
        (block_user, block_slot, block_hour, user_factor, hot_factor, hour_factor, observed),
        (),
        state_of(hot_slots)
        + (shape(blocks, rank_size),)
        + sums
        + (shape(*table_of(hot_slots)), shape(2 * HALF, rank_size, dtype=BF16), row, row, row),
        [
            users_room,
            room(*hot_factor.shape, dtype=BF16),
            room(*hour_factor.shape, dtype=BF16),
            observed_room,
            pltpu.SemaphoreType.DMA((7,)),
        ],
        5 * 10**9,
    )
    hours_tab, slot_row = hot_state[-4], hot_state[-2]
    served = call(
        serve,
        needs if turns <= 8 else [jnp.concatenate(needs, axis=0).reshape(turns, -1)],
        (),
        (cold_factor, theirs),
        (shape(2 * reqs * IB, rank_size, dtype=BF16),) * turns,
        [room(2 * shard_len, rank_size, dtype=BF16)],
        10**6,
    )
    hot_state, served = lax.optimization_barrier((hot_state, served))
    fetched = [served[0]] + [turn(served[m], "users", peers, 2 * m) for m in range(1, turns)]
    needs = jnp.concatenate(needs, axis=0)
    cold_state = call(
        second_kernel,
        (block_count,),
        (user_factor, observed),
        hot_state,
        state_of(cold_slots) + (shape(blocks, rank_size),) + sums,
        [users_room, observed_room, pltpu.SemaphoreType.DMA((2,))],
        5 * 10**9,
    )
    *cold_state, hot_terms, hot_whole, hour_whole = cold_state
    send, keep, returned, cold_terms = call(
        third_kernel,
        (block_count,),
        (),
        (slot_row, hours_tab, *cold_state, hot_whole, hour_whole, *fetched),
        (
            shape(split_hot + 2 * high_rows, rank_size, dtype=BF16),
            shape(split_hot + high_rows, rank_size),
            shape(cold_slots * IB, rank_size, dtype=BF16),
            shape(blocks, rank_size),
        ),
        [room(*table_of(cold_slots)), room(*table_of(cold_slots)), room(2 * HALF, rank_size)],
        5 * 10**9,
    )
    returned = returned.reshape(peers, reqs * IB, rank_size)
    send_user, user = call(
        users_kernel,
        (block_count,),
        (),
        (slot_row, hot_state[5], hot_terms, cold_state[5], cold_terms),
        (shape(users // 2, rank_size, dtype=BF16), shape(users // 2, rank_size)),
        [],
        10**9,
    )

    got = hop(send, "items", items, 0)
    hot = keep[:split_hot] + got[:split_hot].astype(F32)
    hour = keep[split_hot:] + got[split_hot : split_hot + high_rows].astype(F32)
    hour += got[split_hot + high_rows :].astype(F32)
    user += hop(send_user, "items", items, 0).astype(F32)

    steps = [("items", items, bit) for bit in range(1, bits_of(items))]
    steps += [("users", peers, bit) for bit in range(bits_of(peers))]

    def send_back(returned, bit):
        size = returned.shape[0] // 2
        return jnp.concatenate([returned[:size], hop(returned[size:], "users", peers, bit)], axis=1)

    bits = list(range(bits_of(peers)))
    returned = send_back(returned, bits.pop())
    first = bits_of(items) - 1
    for place, step in enumerate(steps):
        last = place == len(steps) - 1
        rows = hot.shape[0] // 2
        high = lax.reduce_precision(hour, 8, 7)
        parts = [hot[rows:].astype(BF16), high.astype(BF16)]
        exact = step[0] == "items"
        if exact:
            parts.append((hour - high).astype(BF16))
        else:
            hour = high
        parts = jnp.concatenate(parts, axis=0)
        if place == first:
            parts, user = lax.optimization_barrier((parts, user))
        if place == first:
            needs = jnp.stack([needs, hop(needs, "users", peers, 0)], axis=1)
        got = hop(parts, *step)
        if place == first:
            for other in steps[:first]:
                rows_user = user.shape[0] // 2
                got_user = hop(user[rows_user:].astype(BF16), *other)
                if other != steps[first - 1]:
                    user = user[:rows_user] + got_user.astype(F32)
        if place % 2 and bits:
            returned = send_back(returned, bits.pop())
        elif not last:
            got, returned = lax.optimization_barrier((got, returned))
        if place == len(steps) - 2:
            got, got_user, needs = lax.optimization_barrier((got, got_user, needs))
        if last:
            got_hot = got[:rows]
            hot = hot[:rows]
            hour = hour + got[rows : rows + high_rows].astype(F32)
            break
        hot = hot[:rows] + got[:rows].astype(F32)
        hour = hour + got[rows : rows + high_rows].astype(F32)
        if exact:
            hour = hour + got[rows + high_rows :].astype(F32)
    while bits:
        returned = send_back(returned, bits.pop())
    user = user[:rows_user] + got_user.astype(F32)
    mine = hour[:half]
    other = hop(mine, "items", items, 0)
    if not permute_hot:
        hot, got_hot = jnp.zeros((IB, rank_size), F32), jnp.zeros((IB, rank_size), BF16)
    cold_grad, hot, hour_grad = call(
        finish,
        (),
        (),
        (needs.reshape(-1, peers), returned.reshape(-1, rank_size), mine, other, hot, got_hot),
        (shape(shard_len, rank_size), shape(hot.shape[0], rank_size), shape(hours, rank_size)),
        [],
        10**8,
    )
    if not permute_hot:
        hot_whole = jnp.concatenate([hot_whole[part] for part in range(hot_whole.shape[0])], axis=1)
        hot = lax.psum_scatter(hot_whole, ("users", "items"), scatter_dimension=0, tiled=True)
    return (user, cold_grad, hot, hour_grad)


def solution(mesh):
    in_specs = (
        P("users", None),
        P(),
        P(("users", "items"), None),
        P(),
        P(("users", "items"), None),
        P(("users", "items"), None),
        P(("users", "items"), None),
        P(("users", "items")),
        P(("users", "items"), None, None),
        P(("users", "items"), None, None),
    )
    out_specs = (
        P(("users", "items"), None),
        P(("users", "items"), None),
        P(("users", "items"), None),
        P(),
    )
    return jax.shard_map(body, mesh=mesh, in_specs=in_specs, out_specs=out_specs, check_vma=False)
```

```python
import collections
import functools

import jax
import jax.numpy as jnp
from jax import lax
from jax.experimental import pallas as pl
from jax.experimental.pallas import tpu as pltpu
from jax.sharding import PartitionSpec as P

IB = 16
HB = 8
HALF = 128
F32 = jnp.float32
BF16 = jnp.bfloat16

Sizes = collections.namedtuple(
    "Sizes",
    ("peers", "items", "hot_slots", "reqs", "hours", "permute_hot", "split_hot", "hot_blocks", "cold_blocks"),
)


def bits_of(size):
    return size.bit_length() - 1


def padded(rows):
    return -(-rows // 16) * 16


def flip(value, bits):
    out = jnp.zeros_like(value)
    for k in range(bits):
        out = out | (((value >> k) & 1) << (bits - 1 - k))
    return out


def hour_of(lane, split, hours):
    half = hours // 2
    inside = lane & (HALF - 1)
    hour = ((lane >> 7) ^ split) * half + inside
    return hour, inside < half


def one_hot(mask):
    return mask.astype(F32).astype(BF16)


def column(row):
    parts = [jnp.transpose(jnp.broadcast_to(row[:, k : k + 128], (128, 128))) for k in range(0, row.shape[1], 128)]
    return jnp.concatenate(parts, axis=0)


def spread(col, lanes):
    return jnp.concatenate([col] * (-(-lanes // 128)), axis=1)[:, :lanes]


def load_table(table, rows, at=0):
    for part in range(table.shape[0]):
        table[part, at : at + rows.shape[0], :] = rows[:, part * 128 : part * 128 + 128].astype(F32)


def chosen_blocks(sizes, hot, count, slot_row):
    place = lax.broadcasted_iota(jnp.int32, slot_row.shape, 1)
    of_kind = (slot_row < sizes.hot_slots) if hot else (slot_row >= sizes.hot_slots)
    chosen = (place < count) & of_kind
    return chosen, jnp.sum(chosen.astype(F32))


def prepare(sizes, hot, m, p, q, chosen, user, slot, hour, user_tab, observed, out):
    obs, live_hour, user_rows, pick, put, user_pos = out
    blocks = slot.shape[1]
    users = user_tab.shape[0]
    user_chunk = users // sizes.items

    kind = jnp.broadcast_to(chosen.astype(F32), (8, blocks)).astype(BF16)
    before = one_hot(
        lax.broadcasted_iota(jnp.int32, (blocks, blocks), 0) < lax.broadcasted_iota(jnp.int32, (blocks, blocks), 1)
    )
    rank = jnp.dot(kind, before, preferred_element_type=F32)[:1]
    rank = jnp.where(chosen, rank, -1.0).astype(jnp.int32)
    order = one_hot(rank == lax.broadcasted_iota(jnp.int32, (m, blocks), 0))
    user_in = user[...]
    rows = [user_in >> 4, user_in & 15, slot[...], hour[...] + 1]
    rows = jnp.concatenate([row.astype(F32) for row in rows] + [jnp.zeros((4, blocks), F32)], axis=0).astype(BF16)
    rows = lax.dot_general(rows, order, (((1,), (1,)), ((), ())), preferred_element_type=F32).astype(jnp.int32)
    user_row, slot_row, hour_row = rows[0:1] * 16 + rows[1:2], rows[2:3], rows[3:4] - 1
    obs[:m, :] = jnp.dot(order, 0.5 - observed[...], preferred_element_type=F32)

    user_col, hour_col = column(user_row), column(hour_row)
    step = 512
    total = jnp.zeros((m, user_tab.shape[1]), F32)
    for k in range(0, users, step):
        lane = lax.broadcasted_iota(jnp.int32, (m, step), 1) + k
        total += jnp.dot(one_hot(spread(user_col, step) == lane), user_tab[k : k + step, :], preferred_element_type=F32)
    user_rows[:m, :] = total

    slots = pick.shape[1]
    if hot:
        put_pos = flip(slot_row ^ (p * sizes.items + q), bits_of(sizes.peers * sizes.items)) if sizes.permute_hot else slot_row
    else:
        owner, request = (slot_row - sizes.hot_slots) // sizes.reqs, (slot_row - sizes.hot_slots) % sizes.reqs
        put_pos = flip(owner ^ p, bits_of(sizes.peers)) * sizes.reqs + request
        slot_row = (owner ^ (p & ~1)) * sizes.reqs + request
    pick[:m, :] = one_hot(spread(column(slot_row), slots) == lax.broadcasted_iota(jnp.int32, (m, slots), 1))
    put[:, :m] = one_hot(put_pos == lax.broadcasted_iota(jnp.int32, (slots, m), 0))
    user_pos[:, :m] = flip((user_row // user_chunk) ^ q, bits_of(sizes.items)) * user_chunk + user_row % user_chunk

    lane = lax.broadcasted_iota(jnp.int32, (m, 2 * HALF), 1)
    lane_hour, used = hour_of(lane, q & 1, sizes.hours)
    live_hour[:m, :] = (used & ((lane_hour // HB) == spread(hour_col, 2 * HALF))).astype(F32)


def work(sizes, m, first, last, q, state, table, hours_tab, user_terms, item_sums, grad_hour, stack=4):
    obs, live_hour, user_rows, pick, put, _ = state
    slots = pick.shape[1]
    parts = range(table.shape[0])
    lane_hour, used = hour_of(lax.broadcasted_iota(jnp.int32, (IB * HB, 2 * HALF), 1), q & 1, sizes.hours)
    cell = lax.broadcasted_iota(jnp.int32, (IB * HB, 2 * HALF), 0)
    tile = one_hot(used & ((cell & (HB - 1)) == (lane_hour & (HB - 1))))
    cell_item = lax.broadcasted_iota(jnp.int32, (m, IB * HB), 1) // HB

    def one(group, carry):
        places = [group * stack + j for j in range(stack)]
        rows, cells = [], []
        for a in places:
            of_place = pl.ds(a, slots, stride=IB)
            choice = jnp.concatenate([table[part, of_place, :] for part in parts], axis=1).astype(BF16)
            rows.append(jnp.dot(pick[:m, :], choice, preferred_element_type=F32))
            cells.append(jnp.where(cell_item == a, obs[:m, :], 0.0).astype(BF16))
        users_f = user_rows[:m, :]
        user_item = jnp.concatenate([(users_f * row).astype(BF16) for row in rows], axis=0)
        half_model = lax.dot_general(
            user_item, hours_tab[...] * jnp.asarray(0.5, BF16), (((1,), (1,)), ((), ())), preferred_element_type=F32
        )
        seen = jnp.dot(jnp.concatenate(cells, axis=0), tile, preferred_element_type=F32)
        live = jnp.concatenate([live_hour[:m, :]] * stack, axis=0)
        residual = ((0.5 * jnp.tanh(half_model) + seen) * live).astype(BF16)
        weighted = jnp.dot(residual, hours_tab[...], preferred_element_type=F32)
        grad_hour[...] += lax.dot_general(
            residual, user_item, (((0,), (0,)), ((), ())), preferred_element_type=F32
        )
        into = put[:, :m]
        total = user_terms[:m, :]
        for j, a in enumerate(places):
            mine = weighted[j * m : j * m + m]
            total += mine * rows[j]
            terms = mine * users_f
            high = terms.astype(BF16)
            low = (terms - high.astype(F32)).astype(BF16)
            sums = jnp.dot(into, high, preferred_element_type=F32) + jnp.dot(into, low, preferred_element_type=F32)
            for part in parts:
                item_sums[part, pl.ds(a, slots, stride=IB), :] = sums[:, part * 128 : part * 128 + 128]
        user_terms[:m, :] = total
        return carry

    lax.fori_loop(first // stack, last // stack, one, 0)


def in_size(number, small, whole, run):
    pl.when(number <= small)(lambda: run(small))
    pl.when(number > small)(lambda: run(whole))


def serve(sizes, *refs):
    turns = sizes.peers // 2
    needs, (mine, theirs), outs, table = refs[: -turns - 3], refs[-turns - 3 : -turns - 1], refs[-turns - 1 : -1], refs[-1]
    p = lax.axis_index("users")
    rows = mine.shape[0]
    table[pl.ds(pl.multiple_of((p & 1) * rows, rows), rows), :] = mine[...]
    table[pl.ds(pl.multiple_of((1 - (p & 1)) * rows, rows), rows), :] = theirs[...]
    for m, out in enumerate(outs):
        for which in range(2):
            for r in range(sizes.reqs):
                owner = (p & ~1) + which
                block = needs[m][0, r, owner] if len(needs) == turns else needs[0][m, r * sizes.peers + owner]
                at = pl.multiple_of(which * rows + block * IB, IB)
                to = (which * sizes.reqs + r) * IB
                out[to : to + IB, :] = table[pl.ds(at, IB), :]


def start_copies(pairs, sems):
    copies = [pltpu.make_async_copy(source, target, sems.at[k]) for k, (source, target) in enumerate(pairs)]
    for copy in copies:
        copy.start()
    return copies


def first_kernel(
    sizes, count, user_in, slot_in, hour_in, user_tab_in, hot_in, hour_factor_in, observed_in,
    obs, live_hour, user_rows, pick, put, user_pos, user_terms, item_sums, grad_hour,
    table, hours_tab, user, slot, hour,
    user_tab, hot, hour_factor, observed, sems,
):
    state = (obs, live_hour, user_rows, pick, put, user_pos)
    p, q = lax.axis_index("users"), lax.axis_index("items")
    sources = (slot_in, user_in, hour_in, observed_in.at[0], user_tab_in, hour_factor_in, hot_in)
    copies = start_copies(zip(sources, (slot, user, hour, observed, user_tab, hour_factor, hot)), sems)
    user_terms[...] = jnp.zeros_like(user_terms)
    grad_hour[...] = jnp.zeros_like(grad_hour)
    for copy in copies[:3]:
        copy.wait()
    chosen, number = chosen_blocks(sizes, True, count[0], slot[...])
    for copy in copies[3:]:
        copy.wait()
    load_table(table, hot)
    row_hour, used = hour_of(lax.broadcasted_iota(jnp.int32, (2 * HALF, sizes.hours), 0), q & 1, sizes.hours)
    hit = one_hot(used & (row_hour == lax.broadcasted_iota(jnp.int32, (2 * HALF, sizes.hours), 1)))
    hours_tab[...] = jnp.dot(hit, hour_factor[...], preferred_element_type=F32).astype(BF16)

    def run(m):
        prepare(sizes, True, m, p, q, chosen, user, slot, hour, user_tab, observed, state)
        work(sizes, m, 0, IB // 4, q, state, table, hours_tab, user_terms, item_sums, grad_hour)

    in_size(number, sizes.hot_blocks, slot.shape[1], run)


def second_kernel(
    sizes, count, user_tab_in, observed_in,
    obs, live_hour, user_rows, pick, put, user_pos, user_terms_in, item_sums_in, grad_hour_in,
    table, hours_tab, user, slot, hour,
    obs_2, live_hour_2, user_rows_2, pick_2, put_2, user_pos_2, user_terms, item_sums, grad_hour,
    user_tab, observed, sems,
):
    state = (obs, live_hour, user_rows, pick, put, user_pos)
    state_2 = (obs_2, live_hour_2, user_rows_2, pick_2, put_2, user_pos_2)
    p, q = lax.axis_index("users"), lax.axis_index("items")
    copies = start_copies(zip((observed_in.at[0], user_tab_in), (observed, user_tab)), sems)
    user_terms[...] = user_terms_in[...]
    item_sums[...] = item_sums_in[...]
    grad_hour[...] = grad_hour_in[...]
    _, number = chosen_blocks(sizes, True, count[0], slot[...])

    def run(m):
        work(sizes, m, IB // 4, IB, q, state, table, hours_tab, user_terms, item_sums, grad_hour)

    in_size(number, sizes.hot_blocks, slot.shape[1], run)
    chosen, number = chosen_blocks(sizes, False, count[0], slot[...])
    for copy in copies:
        copy.wait()

    def make(m):
        prepare(sizes, False, m, p, q, chosen, user, slot, hour, user_tab, observed, state_2)

    in_size(number, sizes.cold_blocks, slot.shape[1], make)


def third_kernel(
    sizes, count, slot, hours_tab,
    obs, live_hour, user_rows, pick, put, user_pos, hot_sums, grad_hour_in,
    *refs,
):
    fetched, (send, keep, cold_send, user_terms, table, item_sums, grad_hour) = refs[:-7], refs[-7:]
    state = (obs, live_hour, user_rows, pick, put, user_pos)
    q = lax.axis_index("items")
    rows = fetched[0].shape[0]
    for m, block in enumerate(fetched):
        load_table(table, block, m * rows)
    user_terms[...] = jnp.zeros_like(user_terms)
    grad_hour[...] = grad_hour_in[...]
    _, number = chosen_blocks(sizes, False, count[0], slot[...])

    def run(m):
        work(sizes, m, 0, IB, q, state, table, hours_tab, user_terms, item_sums, grad_hour, stack=8)

    in_size(number, sizes.cold_blocks, slot.shape[1], run)

    high_rows = padded(sizes.hours // 2)
    at = sizes.split_hot
    for part in range(table.shape[0]):
        lanes = slice(part * 128, part * 128 + 128)
        if at:
            keep[:at, lanes] = hot_sums[part, :at, :]
            send[:at, lanes] = hot_sums[part, at : 2 * at, :].astype(BF16)
        cold_send[:, lanes] = item_sums[part].astype(BF16)
    keep[at : at + high_rows, :] = grad_hour[:high_rows, :]
    other = grad_hour[HALF : HALF + high_rows, :]
    high = other.astype(BF16)
    send[at : at + high_rows, :] = high
    send[at + high_rows : at + 2 * high_rows, :] = (other - high.astype(F32)).astype(BF16)


def users_kernel(sizes, count, slot, pos, terms, pos_2, terms_2, send, keep, step=256):
    _, number = chosen_blocks(sizes, True, count[0], slot[...])
    _, number_2 = chosen_blocks(sizes, False, count[0], slot[...])

    def add(m, m_2):
        total = jnp.concatenate([terms[:m, :], terms_2[:m_2, :]], axis=0)
        high = total.astype(BF16)
        low = (total - high.astype(F32)).astype(BF16)
        row = jnp.concatenate([pos[:, :m], pos_2[:, :m_2]], axis=1)
        within = one_hot((row & (step - 1)) == lax.broadcasted_iota(jnp.int32, (step, m + m_2), 0))
        for k in range(0, 2 * keep.shape[0], step):
            hit = within * one_hot((row // step) == k // step)
            sums = jnp.dot(hit, high, preferred_element_type=F32) + jnp.dot(hit, low, preferred_element_type=F32)
            if k < keep.shape[0]:
                keep[k : k + step, :] = sums
            else:
                send[k - keep.shape[0] : k - keep.shape[0] + step, :] = sums.astype(BF16)

    def hot(m):
        in_size(number_2, sizes.cold_blocks, slot.shape[1], lambda m_2: add(m, m_2))

    in_size(number, sizes.hot_blocks, slot.shape[1], hot)


def finish(sizes, needs, returned, mine, other, hot, got, cold_grad, hot_grad, hour_grad):
    p, q = lax.axis_index("users"), lax.axis_index("items")
    hot_grad[...] = hot[...] + got[...].astype(F32)
    half = mine.shape[0]
    swap = (q & 1) == 1
    hour_grad[:half, :] = jnp.where(swap, other[...], mine[...])
    hour_grad[half:, :] = jnp.where(swap, mine[...], other[...])
    asked, rows = needs.shape[0], returned.shape[0]
    lane = lax.broadcasted_iota(jnp.int32, needs.shape, 1)
    mask = jnp.where(lane == p, needs[...], 0).astype(F32)
    wanted = jnp.broadcast_to(jnp.sum(mask, axis=1, keepdims=True), (asked, 128)).astype(BF16)
    number = lax.broadcasted_iota(jnp.int32, (asked, rows), 1) // IB
    place = one_hot(number == lax.broadcasted_iota(jnp.int32, (asked, rows), 0))
    block = lax.dot_general(wanted, place, (((0,), (0,)), ((), ())), preferred_element_type=F32)[:1].astype(jnp.int32)
    size = (cold_grad.shape[0], rows)
    row, column = lax.broadcasted_iota(jnp.int32, size, 0), lax.broadcasted_iota(jnp.int32, size, 1)
    hit = one_hot((row // IB == block) & (row % IB == column % IB))
    cold_grad[...] = jnp.dot(hit, returned[...], preferred_element_type=F32)


def hop(values, axis, size, bit):
    return lax.ppermute(values, axis, [(i, i ^ (1 << bit)) for i in range(size)])


def turn(values, axis, size, change):
    return lax.ppermute(values, axis, [(i, i ^ change) for i in range(size)])


def halves(values):
    rows = values.shape[0] // 2
    return values[:rows], values[rows:]


def body(
    user_factor,
    hot_factor,
    cold_factor,
    hour_factor,
    block_user,
    block_slot,
    block_hour,
    block_count,
    need_rows,
    observed,
):
    rank_size = user_factor.shape[1]
    hours = hour_factor.shape[0]
    hot_rows = hot_factor.shape[0]
    shard_len = cold_factor.shape[0]
    peers, items = lax.axis_size("users"), lax.axis_size("items")
    reqs = need_rows.shape[2]
    half = hours // 2
    blocks = block_user.shape[1]
    users = user_factor.shape[0]
    hot_slots, cold_slots = hot_rows // IB, peers * reqs
    permute_hot = hot_rows == IB * peers * items
    high_rows = padded(half)
    split_hot = hot_rows // 2 if permute_hot else 0
    sizes = Sizes(
        peers, items, hot_slots, reqs, hours, permute_hot, split_hot, blocks // 4 * 3, blocks // 2
    )
    vmem = pl.BlockSpec(memory_space=pltpu.VMEM)
    smem = pl.BlockSpec(memory_space=pltpu.SMEM)
    hbm = pl.BlockSpec(memory_space=pltpu.HBM)

    def shape(*dims, dtype=F32):
        return jax.ShapeDtypeStruct(dims, dtype)

    def state_of(slots):
        return (
            shape(blocks, IB * HB),
            shape(blocks, 2 * HALF),
            shape(blocks, rank_size),
            shape(blocks, slots, dtype=BF16),
            shape(slots, blocks, dtype=BF16),
            shape(1, blocks, dtype=jnp.int32),
        )

    def table_of(slots):
        return (rank_size // 128, slots * IB, 128)

    def call(function, scalar, far, near, out_shape, scratch, flops):
        return pl.pallas_call(
            functools.partial(function, sizes),
            out_shape=out_shape,
            in_specs=[smem] * len(scalar) + [hbm] * len(far) + [vmem] * len(near),
            out_specs=(vmem,) * len(out_shape),
            scratch_shapes=scratch,
            compiler_params=pltpu.CompilerParams(vmem_limit_bytes=24 * 1024 * 1024),
            cost_estimate=pl.CostEstimate(flops=flops, bytes_accessed=4 << 20, transcendentals=0),
            name=function.__name__,
        )(*scalar, *[pltpu.with_memory_space_constraint(value, pltpu.HBM) for value in far], *near)

    turns = peers // 2
    theirs = hop(cold_factor, "users", peers, 0)
    need = jnp.transpose(need_rows, (0, 2, 1))
    needs = [need] + [turn(need, "users", peers, 2 * m) for m in range(1, turns)]

    def room(*dims, dtype=F32):
        return pltpu.VMEM(dims, dtype)

    row = shape(1, blocks, dtype=jnp.int32)
    sums = (shape(*table_of(hot_slots)), shape(2 * HALF, rank_size))
    users_room = room(*user_factor.shape, dtype=BF16)
    observed_room = room(*observed.shape[1:], dtype=BF16)
    hot_state = call(
        first_kernel,
        (block_count,),
        (block_user, block_slot, block_hour, user_factor, hot_factor, hour_factor, observed),
        (),
        state_of(hot_slots)
        + (shape(blocks, rank_size),)
        + sums
        + (shape(*table_of(hot_slots)), shape(2 * HALF, rank_size, dtype=BF16), row, row, row),
        [
            users_room,
            room(*hot_factor.shape, dtype=BF16),
            room(*hour_factor.shape, dtype=BF16),
            observed_room,
            pltpu.SemaphoreType.DMA((7,)),
        ],
        10**8,
    )
    hours_tab, slot_row = hot_state[-4], hot_state[-2]
    served = call(
        serve,
        needs if turns <= 8 else [jnp.concatenate(needs, axis=0).reshape(turns, -1)],
        (),
        (cold_factor, theirs),
        (shape(2 * reqs * IB, rank_size, dtype=BF16),) * turns,
        [room(2 * shard_len, rank_size, dtype=BF16)],
        10**6,
    )
    hot_state, served = lax.optimization_barrier((hot_state, served))
    fetched = [served[0]] + [turn(served[m], "users", peers, 2 * m) for m in range(1, turns)]
    needs = jnp.concatenate(needs, axis=0)
    cold_state = call(
        second_kernel,
        (block_count,),
        (user_factor, observed),
        hot_state,
        state_of(cold_slots) + (shape(blocks, rank_size),) + sums,
        [users_room, observed_room, pltpu.SemaphoreType.DMA((2,))],
        5 * 10**9,
    )
    *cold_state, hot_terms, hot_whole, hour_whole = cold_state
    send, keep, returned, cold_terms = call(
        third_kernel,
        (block_count,),
        (),
        (slot_row, hours_tab, *cold_state, hot_whole, hour_whole, *fetched),
        (
            shape(split_hot + 2 * high_rows, rank_size, dtype=BF16),
            shape(split_hot + high_rows, rank_size),
            shape(cold_slots * IB, rank_size, dtype=BF16),
            shape(blocks, rank_size),
        ),
        [room(*table_of(cold_slots)), room(*table_of(cold_slots)), room(2 * HALF, rank_size)],
        5 * 10**9,
    )
    returned = returned.reshape(peers, reqs * IB, rank_size)
    got = hop(send, "items", items, 0)
    got, cold_terms = lax.optimization_barrier((got, cold_terms))
    hot = keep[:split_hot] + got[:split_hot].astype(F32)
    hour = keep[split_hot:] + got[split_hot : split_hot + high_rows].astype(F32)
    hour += got[split_hot + high_rows :].astype(F32)
    send_user, user = call(
        users_kernel,
        (block_count,),
        (),
        (slot_row, hot_state[5], hot_terms, cold_state[5], cold_terms),
        (shape(users // 2, rank_size, dtype=BF16), shape(users // 2, rank_size)),
        [],
        10**9,
    )

    user += hop(send_user, "items", items, 0).astype(F32)
    rows = hot.shape[0] // 4
    high = lax.reduce_precision(hour, 8, 7)
    whole = high.astype(BF16)
    parts = [[hot[k * rows : (k + 1) * rows].astype(BF16), whole] for k in range(1, 4)]
    size = returned.shape[0] // 2
    parts[0].append(returned[size:].reshape(-1, rank_size))
    changes = (items, 2, items + 2)
    got = [
        turn(jnp.concatenate(part, axis=0), ("users", "items"), peers * items, change)
        for part, change in zip(parts, changes)
    ]
    back = got[0][rows + high_rows :]
    returned = jnp.concatenate([returned[:size], back.reshape(returned[:size].shape)], axis=1)
    got = [one[: rows + high_rows] for one in got]
    hot = hot[:rows] + sum(one[:rows].astype(F32) for one in got)
    by_user, by_item, by_both = [one[rows:].astype(F32) for one in got]
    hour = (high + by_item) + (by_user + by_both)

    last = bits_of(peers) - 1
    for bit in range(1, bits_of(peers)):
        rows, size = hot.shape[0] // 2, returned.shape[0] // 2
        high = lax.reduce_precision(hour, 8, 7)
        parts = [hot[rows:].astype(BF16), high.astype(BF16), returned[size:].reshape(-1, rank_size)]
        parts = jnp.concatenate(parts, axis=0)
        if bit == 1:
            parts, user, needs = lax.optimization_barrier((parts, user, needs))
        got = hop(parts, "users", peers, bit)
        if bit == 1:
            keep_user = user.shape[0] // 2
            got_user = hop(user[keep_user:].astype(BF16), "items", items, 1)
            needs = jnp.stack([needs, hop(needs, "users", peers, 0)], axis=1)
        if bit == last:
            got, got_user, needs = lax.optimization_barrier((got, got_user, needs))
        back = got[rows + high_rows :]
        returned = jnp.concatenate([returned[:size], back.reshape(returned[:size].shape)], axis=1)
        hour = high + got[rows : rows + high_rows].astype(F32)
        if bit < last:
            hot = hot[:rows] + got[:rows].astype(F32)
    hot, got_hot = hot[:rows], got[:rows]
    user = user[:keep_user] + got_user.astype(F32)
    mine = hour[:half]
    other = hop(mine, "items", items, 0)
    if not permute_hot:
        hot, got_hot = jnp.zeros((IB, rank_size), F32), jnp.zeros((IB, rank_size), BF16)
    cold_grad, hot, hour_grad = call(
        finish,
        (),
        (),
        (needs.reshape(-1, peers), returned.reshape(-1, rank_size), mine, other, hot, got_hot),
        (shape(shard_len, rank_size), shape(hot.shape[0], rank_size), shape(hours, rank_size)),
        [],
        10**8,
    )
    if not permute_hot:
        hot_whole = jnp.concatenate([hot_whole[part] for part in range(hot_whole.shape[0])], axis=1)
        hot = lax.psum_scatter(hot_whole, ("users", "items"), scatter_dimension=0, tiled=True)
    return (user, cold_grad, hot, hour_grad)


def solution(mesh):
    in_specs = (
        P("users", None),
        P(),
        P(("users", "items"), None),
        P(),
        P(("users", "items"), None),
        P(("users", "items"), None),
        P(("users", "items"), None),
        P(("users", "items")),
        P(("users", "items"), None, None),
        P(("users", "items"), None, None),
    )
    out_specs = (
        P(("users", "items"), None),
        P(("users", "items"), None),
        P(("users", "items"), None),
        P(),
    )
    return jax.shard_map(body, mesh=mesh, in_specs=in_specs, out_specs=out_specs, check_vma=False)
```

```python
import collections
import functools

import jax
import jax.numpy as jnp
from jax import lax
from jax.experimental import pallas as pl
from jax.experimental.pallas import tpu as pltpu
from jax.sharding import PartitionSpec as P

IB = 16
HB = 8
HALF = 128
F32 = jnp.float32
BF16 = jnp.bfloat16

Sizes = collections.namedtuple(
    "Sizes",
    ("peers", "items", "hot_slots", "reqs", "hours", "permute_hot", "split_hot", "hot_blocks", "cold_blocks"),
)


def bits_of(size):
    return size.bit_length() - 1


def padded(rows):
    return -(-rows // 16) * 16


def flip(value, bits):
    out = jnp.zeros_like(value)
    for k in range(bits):
        out = out | (((value >> k) & 1) << (bits - 1 - k))
    return out


def hour_of(lane, split, hours):
    half = hours // 2
    inside = lane & (HALF - 1)
    hour = ((lane >> 7) ^ split) * half + inside
    return hour, inside < half


def one_hot(mask):
    return mask.astype(F32).astype(BF16)


def column(row):
    parts = [jnp.transpose(jnp.broadcast_to(row[:, k : k + 128], (128, 128))) for k in range(0, row.shape[1], 128)]
    return jnp.concatenate(parts, axis=0)


def spread(col, lanes):
    return jnp.concatenate([col] * (-(-lanes // 128)), axis=1)[:, :lanes]


def load_table(table, rows, at=0):
    for part in range(table.shape[0]):
        table[part, at : at + rows.shape[0], :] = rows[:, part * 128 : part * 128 + 128].astype(F32)


def chosen_blocks(sizes, hot, count, slot_row):
    place = lax.broadcasted_iota(jnp.int32, slot_row.shape, 1)
    of_kind = (slot_row < sizes.hot_slots) if hot else (slot_row >= sizes.hot_slots)
    chosen = (place < count) & of_kind
    return chosen, jnp.sum(chosen.astype(F32))


def prepare(sizes, hot, m, p, q, chosen, user, slot, hour, user_tab, observed, out, users_here=None):
    obs, live_hour, user_rows, pick, put, user_pos = out
    blocks = slot.shape[1]
    users = user_tab.shape[0]
    user_chunk = users // sizes.items

    kind = jnp.broadcast_to(chosen.astype(F32), (8, blocks)).astype(BF16)
    before = one_hot(
        lax.broadcasted_iota(jnp.int32, (blocks, blocks), 0) < lax.broadcasted_iota(jnp.int32, (blocks, blocks), 1)
    )
    rank = jnp.dot(kind, before, preferred_element_type=F32)[:1]
    rank = jnp.where(chosen, rank, -1.0).astype(jnp.int32)
    order = one_hot(rank == lax.broadcasted_iota(jnp.int32, (m, blocks), 0))
    user_in = user[...]
    rows = [user_in >> 4, user_in & 15, slot[...], hour[...] + 1]
    rows = jnp.concatenate([row.astype(F32) for row in rows] + [jnp.zeros((4, blocks), F32)], axis=0).astype(BF16)
    rows = lax.dot_general(rows, order, (((1,), (1,)), ((), ())), preferred_element_type=F32).astype(jnp.int32)
    user_row, slot_row, hour_row = rows[0:1] * 16 + rows[1:2], rows[2:3], rows[3:4] - 1
    obs[:m, :] = jnp.dot(order, 0.5 - observed[...], preferred_element_type=F32)

    user_col, hour_col = column(user_row), column(hour_row)
    if users_here is not None:
        users_here.wait()
    step = 512
    total = jnp.zeros((m, user_tab.shape[1]), F32)
    for k in range(0, users, step):
        lane = lax.broadcasted_iota(jnp.int32, (m, step), 1) + k
        total += jnp.dot(one_hot(spread(user_col, step) == lane), user_tab[k : k + step, :], preferred_element_type=F32)
    user_rows[:m, :] = total

    slots = pick.shape[1]
    if hot:
        put_pos = flip(slot_row ^ (p * sizes.items + q), bits_of(sizes.peers * sizes.items)) if sizes.permute_hot else slot_row
    else:
        owner, request = (slot_row - sizes.hot_slots) // sizes.reqs, (slot_row - sizes.hot_slots) % sizes.reqs
        put_pos = flip(owner ^ p, bits_of(sizes.peers)) * sizes.reqs + request
        slot_row = (owner ^ (p & ~1)) * sizes.reqs + request
    pick[:m, :] = one_hot(spread(column(slot_row), slots) == lax.broadcasted_iota(jnp.int32, (m, slots), 1))
    put[:, :m] = one_hot(put_pos == lax.broadcasted_iota(jnp.int32, (slots, m), 0))
    user_pos[:, :m] = flip((user_row // user_chunk) ^ q, bits_of(sizes.items)) * user_chunk + user_row % user_chunk

    lane = lax.broadcasted_iota(jnp.int32, (m, 2 * HALF), 1)
    lane_hour, used = hour_of(lane, q & 1, sizes.hours)
    live_hour[:m, :] = (used & ((lane_hour // HB) == spread(hour_col, 2 * HALF))).astype(F32)


def work(sizes, m, first, last, q, state, table, hours_tab, user_terms, item_sums, grad_hour, before=None, stack=8):
    obs, live_hour, user_rows, pick, put, _ = state
    slots = pick.shape[1]
    parts = range(table.shape[0])
    lane_hour, used = hour_of(lax.broadcasted_iota(jnp.int32, (IB * HB, 2 * HALF), 1), q & 1, sizes.hours)
    cell = lax.broadcasted_iota(jnp.int32, (IB * HB, 2 * HALF), 0)
    tile = one_hot(used & ((cell & (HB - 1)) == (lane_hour & (HB - 1))))
    cell_item = lax.broadcasted_iota(jnp.int32, (m, IB * HB), 1) // HB

    def one(group, terms_before, hours_before):
        places = [group * stack + j for j in range(stack)]
        rows, cells = [], []
        for a in places:
            of_place = pl.ds(a, slots, stride=IB)
            choice = jnp.concatenate([table[part, of_place, :] for part in parts], axis=1).astype(BF16)
            rows.append(jnp.dot(pick[:m, :], choice, preferred_element_type=F32))
            cells.append(jnp.where(cell_item == a, obs[:m, :], 0.0).astype(BF16))
        users_f = user_rows[:m, :]
        user_item = jnp.concatenate([(users_f * row).astype(BF16) for row in rows], axis=0)
        half_model = lax.dot_general(
            user_item, hours_tab[...] * jnp.asarray(0.5, BF16), (((1,), (1,)), ((), ())), preferred_element_type=F32
        )
        seen = jnp.dot(jnp.concatenate(cells, axis=0), tile, preferred_element_type=F32)
        live = jnp.concatenate([live_hour[:m, :]] * stack, axis=0)
        residual = ((0.5 * jnp.tanh(half_model) + seen) * live).astype(BF16)
        weighted = jnp.dot(residual, hours_tab[...], preferred_element_type=F32)
        hour_terms = lax.dot_general(residual, user_item, (((0,), (0,)), ((), ())), preferred_element_type=F32)
        grad_hour[...] = hour_terms + hours_before
        into = put[:, :m]
        total = terms_before
        for j, a in enumerate(places):
            mine = weighted[j * m : j * m + m]
            total += mine * rows[j]
            terms = mine * users_f
            high = terms.astype(BF16)
            low = (terms - high.astype(F32)).astype(BF16)
            sums = jnp.dot(into, high, preferred_element_type=F32) + jnp.dot(into, low, preferred_element_type=F32)
            for part in parts:
                item_sums[part, pl.ds(a, slots, stride=IB), :] = sums[:, part * 128 : part * 128 + 128]
        user_terms[:m, :] = total

    def next_one(group, carry):
        one(group, user_terms[:m, :], grad_hour[...])
        return carry

    if before is not None and last - first == stack:
        one(first // stack, *[0.0 if ref is None else ref[: size or ref.shape[0], :] for ref, size in zip(before, (m, None))])
    else:
        lax.fori_loop(first // stack, last // stack, next_one, 0)


def in_size(number, small, whole, run):
    small = small if isinstance(small, tuple) else (small,)
    pl.when(number <= small[0])(lambda: run(small[0]))
    for below, m in zip(small, small[1:]):
        pl.when((number > below) & (number <= m))(functools.partial(run, m))
    pl.when(number > small[-1])(lambda: run(whole))


def serve(sizes, *refs):
    turns = sizes.peers // 2
    needs, (mine, theirs), outs, table = refs[: -turns - 3], refs[-turns - 3 : -turns - 1], refs[-turns - 1 : -1], refs[-1]
    needs = [(need, k) for need in needs for k in range(need.shape[0])]
    p = lax.axis_index("users")
    rows = mine.shape[0]
    table[pl.ds(pl.multiple_of((p & 1) * rows, rows), rows), :] = mine[...]
    table[pl.ds(pl.multiple_of((1 - (p & 1)) * rows, rows), rows), :] = theirs[...]
    for m, out in enumerate(outs):
        for which in range(2):
            for r in range(sizes.reqs):
                owner = (p & ~1) + which
                block = needs[m][0][needs[m][1], r, owner]
                at = pl.multiple_of(which * rows + block * IB, IB)
                to = (which * sizes.reqs + r) * IB
                out[to : to + IB, :] = table[pl.ds(at, IB), :]


def start_copies(pairs, sems):
    copies = [pltpu.make_async_copy(source, target, sems.at[k]) for k, (source, target) in enumerate(pairs)]
    for copy in copies:
        copy.start()
    return copies


def first_kernel(
    sizes, count, user_in, slot_in, hour_in, user_tab_in, hot_in, hour_factor_in, observed_in,
    obs, live_hour, user_rows, pick, put, user_pos, table, hours_tab, user, slot, hour,
    user_tab, hot, hour_factor, observed, sems,
):
    state = (obs, live_hour, user_rows, pick, put, user_pos)
    p, q = lax.axis_index("users"), lax.axis_index("items")
    sources = (slot_in, user_in, hour_in, observed_in.at[0], hour_factor_in, hot_in, user_tab_in)
    copies = start_copies(zip(sources, (slot, user, hour, observed, hour_factor, hot, user_tab)), sems)
    for copy in copies[:3]:
        copy.wait()
    chosen, number = chosen_blocks(sizes, True, count[0], slot[...])
    for copy in copies[3:-1]:
        copy.wait()
    load_table(table, hot)
    row_hour, used = hour_of(lax.broadcasted_iota(jnp.int32, (2 * HALF, sizes.hours), 0), q & 1, sizes.hours)
    hit = one_hot(used & (row_hour == lax.broadcasted_iota(jnp.int32, (2 * HALF, sizes.hours), 1)))
    hours_tab[...] = jnp.dot(hit, hour_factor[...], preferred_element_type=F32).astype(BF16)

    def run(m):
        prepare(sizes, True, m, p, q, chosen, user, slot, hour, user_tab, observed, state, copies[-1])

    in_size(number, sizes.hot_blocks, slot.shape[1], run)


def half_kernel(
    sizes, count, obs, live_hour, user_rows, pick, put, user_pos, table, hours_tab, slot,
    user_terms, item_sums, grad_hour,
):
    state = (obs, live_hour, user_rows, pick, put, user_pos)
    q = lax.axis_index("items")
    _, number = chosen_blocks(sizes, True, count[0], slot[...])

    def run(m):
        before = (None, None)
        work(sizes, m, 0, IB // 2, q, state, table, hours_tab, user_terms, item_sums, grad_hour, before)

    in_size(number, (sizes.hot_blocks * 11 // 12, sizes.hot_blocks), slot.shape[1], run)


def second_kernel(
    sizes, count, user_tab_in, observed_in,
    obs, live_hour, user_rows, pick, put, user_pos, table, hours_tab, user, slot, hour,
    user_terms_in, item_sums_in, grad_hour_in,
    obs_2, live_hour_2, user_rows_2, pick_2, put_2, user_pos_2, user_terms, item_sums, grad_hour,
    user_tab, observed, sems,
):
    state = (obs, live_hour, user_rows, pick, put, user_pos)
    state_2 = (obs_2, live_hour_2, user_rows_2, pick_2, put_2, user_pos_2)
    p, q = lax.axis_index("users"), lax.axis_index("items")
    copies = start_copies(zip((observed_in.at[0], user_tab_in), (observed, user_tab)), sems)
    item_sums[...] = item_sums_in[...]
    _, number = chosen_blocks(sizes, True, count[0], slot[...])

    def run(m):
        before = (user_terms_in, grad_hour_in)
        work(sizes, m, IB // 2, IB, q, state, table, hours_tab, user_terms, item_sums, grad_hour, before)
        if m < user_terms.shape[0]:
            user_terms[m:, :] = jnp.zeros_like(user_terms[m:, :])

    in_size(number, (sizes.hot_blocks * 11 // 12, sizes.hot_blocks), slot.shape[1], run)
    chosen, number = chosen_blocks(sizes, False, count[0], slot[...])
    for copy in copies:
        copy.wait()

    def make(m):
        prepare(sizes, False, m, p, q, chosen, user, slot, hour, user_tab, observed, state_2)

    in_size(number, sizes.cold_blocks, slot.shape[1], make)


def third_kernel(
    sizes, count, slot, hours_tab,
    obs, live_hour, user_rows, pick, put, user_pos, hot_sums, grad_hour_in,
    *refs,
):
    fetched, (send, keep, cold_send, user_terms, table, item_sums, grad_hour) = refs[:-7], refs[-7:]
    state = (obs, live_hour, user_rows, pick, put, user_pos)
    q = lax.axis_index("items")
    rows = fetched[0].shape[0]
    for m, block in enumerate(fetched):
        load_table(table, block, m * rows)
    user_terms[...] = jnp.zeros_like(user_terms)
    grad_hour[...] = grad_hour_in[...]
    _, number = chosen_blocks(sizes, False, count[0], slot[...])

    def run(m):
        work(sizes, m, 0, IB, q, state, table, hours_tab, user_terms, item_sums, grad_hour)

    in_size(number, (sizes.cold_blocks // 4 * 3, sizes.cold_blocks), slot.shape[1], run)

    high_rows = padded(sizes.hours // 2)
    at = sizes.split_hot
    for part in range(table.shape[0]):
        lanes = slice(part * 128, part * 128 + 128)
        if at:
            keep[:at, lanes] = hot_sums[part, :at, :]
            send[:at, lanes] = hot_sums[part, at : 2 * at, :].astype(BF16)
        cold_send[:, lanes] = item_sums[part].astype(BF16)
    keep[at : at + high_rows, :] = grad_hour[:high_rows, :]
    other = grad_hour[HALF : HALF + high_rows, :]
    high = other.astype(BF16)
    send[at : at + high_rows, :] = high
    send[at + high_rows : at + 2 * high_rows, :] = (other - high.astype(F32)).astype(BF16)


def users_kernel(sizes, count, slot, pos, terms, pos_2, terms_2, send, keep, step=256):
    _, number = chosen_blocks(sizes, True, count[0], slot[...])
    _, number_2 = chosen_blocks(sizes, False, count[0], slot[...])

    def add(m, m_2):
        total = jnp.concatenate([terms[:m, :], terms_2[:m_2, :]], axis=0)
        high = total.astype(BF16)
        low = (total - high.astype(F32)).astype(BF16)
        row = jnp.concatenate([pos[:, :m], pos_2[:, :m_2]], axis=1)
        within = one_hot((row & (step - 1)) == lax.broadcasted_iota(jnp.int32, (step, m + m_2), 0))
        for k in range(0, 2 * keep.shape[0], step):
            hit = within * one_hot((row // step) == k // step)
            sums = jnp.dot(hit, high, preferred_element_type=F32) + jnp.dot(hit, low, preferred_element_type=F32)
            if k < keep.shape[0]:
                keep[k : k + step, :] = sums
            else:
                send[k - keep.shape[0] : k - keep.shape[0] + step, :] = sums.astype(BF16)

    def hot(m):
        in_size(number_2, sizes.cold_blocks, slot.shape[1], lambda m_2: add(m, m_2))

    in_size(number, sizes.hot_blocks, slot.shape[1], hot)


def last_hours(sizes, mine, other, hour_grad):
    half = mine.shape[0]
    swap = (lax.axis_index("items") & 1) == 1
    hour_grad[:half, :] = jnp.where(swap, other[...], mine[...])
    hour_grad[half:, :] = jnp.where(swap, mine[...], other[...])


def last_rows(sizes, needs, returned, hot, got, cold_grad, hot_grad):
    p = lax.axis_index("users")
    hot_grad[...] = hot[...] + got[...].astype(F32)
    asked, rows = needs.shape[0], returned.shape[0]
    lane = lax.broadcasted_iota(jnp.int32, needs.shape, 1)
    mask = jnp.where(lane == p, needs[...], 0).astype(F32)
    wanted = jnp.broadcast_to(jnp.sum(mask, axis=1, keepdims=True), (asked, 128)).astype(BF16)
    number = lax.broadcasted_iota(jnp.int32, (asked, rows), 1) // IB
    place = one_hot(number == lax.broadcasted_iota(jnp.int32, (asked, rows), 0))
    block = lax.dot_general(wanted, place, (((0,), (0,)), ((), ())), preferred_element_type=F32)[:1].astype(jnp.int32)
    size = (cold_grad.shape[0], rows)
    row, column = lax.broadcasted_iota(jnp.int32, size, 0), lax.broadcasted_iota(jnp.int32, size, 1)
    hit = one_hot((row // IB == block) & (row % IB == column % IB))
    cold_grad[...] = jnp.dot(hit, returned[...], preferred_element_type=F32)


def hop(values, axis, size, bit):
    return lax.ppermute(values, axis, [(i, i ^ (1 << bit)) for i in range(size)])


def turn(values, axis, size, change):
    return lax.ppermute(values, axis, [(i, i ^ change) for i in range(size)])


def halves(values):
    rows = values.shape[0] // 2
    return values[:rows], values[rows:]


def body(
    user_factor,
    hot_factor,
    cold_factor,
    hour_factor,
    block_user,
    block_slot,
    block_hour,
    block_count,
    need_rows,
    observed,
):
    rank_size = user_factor.shape[1]
    hours = hour_factor.shape[0]
    hot_rows = hot_factor.shape[0]
    shard_len = cold_factor.shape[0]
    peers, items = lax.axis_size("users"), lax.axis_size("items")
    reqs = need_rows.shape[2]
    half = hours // 2
    blocks = block_user.shape[1]
    users = user_factor.shape[0]
    hot_slots, cold_slots = hot_rows // IB, peers * reqs
    permute_hot = hot_rows == IB * peers * items
    high_rows = padded(half)
    split_hot = hot_rows // 2 if permute_hot else 0
    sizes = Sizes(
        peers, items, hot_slots, reqs, hours, permute_hot, split_hot, blocks // 4 * 3, blocks // 2
    )
    vmem = pl.BlockSpec(memory_space=pltpu.VMEM)
    smem = pl.BlockSpec(memory_space=pltpu.SMEM)
    hbm = pl.BlockSpec(memory_space=pltpu.HBM)

    def shape(*dims, dtype=F32):
        return jax.ShapeDtypeStruct(dims, dtype)

    def state_of(slots):
        return (
            shape(blocks, IB * HB),
            shape(blocks, 2 * HALF),
            shape(blocks, rank_size),
            shape(blocks, slots, dtype=BF16),
            shape(slots, blocks, dtype=BF16),
            shape(1, blocks, dtype=jnp.int32),
        )

    def table_of(slots):
        return (rank_size // 128, slots * IB, 128)

    def call(function, scalar, far, near, out_shape, scratch, flops):
        return pl.pallas_call(
            functools.partial(function, sizes),
            out_shape=out_shape,
            in_specs=[smem] * len(scalar) + [hbm] * len(far) + [vmem] * len(near),
            out_specs=(vmem,) * len(out_shape),
            scratch_shapes=scratch,
            compiler_params=pltpu.CompilerParams(vmem_limit_bytes=24 * 1024 * 1024),
            cost_estimate=pl.CostEstimate(flops=flops, bytes_accessed=4 << 20, transcendentals=0),
            name=function.__name__,
        )(*scalar, *[pltpu.with_memory_space_constraint(value, pltpu.HBM) for value in far], *near)

    turns = peers // 2
    theirs = hop(cold_factor, "users", peers, 0)
    need = jnp.transpose(need_rows, (0, 2, 1))
    needs = [need, hop(need, "users", peers, 1)]

    def room(*dims, dtype=F32):
        return pltpu.VMEM(dims, dtype)

    row = shape(1, blocks, dtype=jnp.int32)
    sums = (shape(*table_of(hot_slots)), shape(2 * HALF, rank_size))
    users_room = room(*user_factor.shape, dtype=BF16)
    observed_room = room(*observed.shape[1:], dtype=BF16)
    hot_state = call(
        first_kernel,
        (block_count,),
        (block_user, block_slot, block_hour, user_factor, hot_factor, hour_factor, observed),
        (),
        state_of(hot_slots) + (shape(*table_of(hot_slots)), shape(2 * HALF, rank_size, dtype=BF16), row, row, row),
        [
            users_room,
            room(*hot_factor.shape, dtype=BF16),
            room(*hour_factor.shape, dtype=BF16),
            observed_room,
            pltpu.SemaphoreType.DMA((7,)),
        ],
        10**8,
    )
    hours_tab, slot_row = hot_state[-4], hot_state[-2]
    needs, hot_state, theirs = lax.optimization_barrier((needs, hot_state, theirs))
    for bit in range(2, bits_of(peers)):
        needs.append(hop(jnp.concatenate(needs, axis=0), "users", peers, bit))
    terms = (shape(blocks, rank_size),) + sums
    hot_sums = call(half_kernel, (block_count,), (), (*hot_state[:8], slot_row), terms, [], 3 * 10**9)
    served = call(
        serve,
        needs,
        (),
        (cold_factor, theirs),
        (shape(2 * reqs * IB, rank_size, dtype=BF16),) * turns,
        [room(2 * shard_len, rank_size, dtype=BF16)],
        10**6,
    )
    hot_state, hot_sums, served = lax.optimization_barrier((hot_state, hot_sums, served))
    fetched = [served[0]] + [turn(served[m], "users", peers, 2 * m) for m in range(1, turns)]
    needs = jnp.concatenate(needs, axis=0)
    cold_state = call(
        second_kernel,
        (block_count,),
        (user_factor, observed),
        (*hot_state, *hot_sums),
        state_of(cold_slots) + terms,
        [users_room, observed_room, pltpu.SemaphoreType.DMA((2,))],
        5 * 10**9,
    )
    *cold_state, hot_terms, hot_whole, hour_whole = cold_state
    send, keep, returned, cold_terms = call(
        third_kernel,
        (block_count,),
        (),
        (slot_row, hours_tab, *cold_state, hot_whole, hour_whole, *fetched),
        (
            shape(split_hot + 2 * high_rows, rank_size, dtype=BF16),
            shape(split_hot + high_rows, rank_size),
            shape(cold_slots * IB, rank_size, dtype=BF16),
            shape(blocks, rank_size),
        ),
        [room(*table_of(cold_slots)), room(*table_of(cold_slots)), room(2 * HALF, rank_size)],
        5 * 10**9,
    )
    returned = returned.reshape(peers, reqs * IB, rank_size)
    got = hop(send, "items", items, 0)
    got, cold_terms = lax.optimization_barrier((got, cold_terms))
    hot = keep[:split_hot] + got[:split_hot].astype(F32)
    hour = keep[split_hot:] + got[split_hot : split_hot + high_rows].astype(F32)
    hour += got[split_hot + high_rows :].astype(F32)
    send_user, user = call(
        users_kernel,
        (block_count,),
        (),
        (slot_row, hot_state[5], hot_terms, cold_state[5], cold_terms),
        (shape(users // 2, rank_size, dtype=BF16), shape(users // 2, rank_size)),
        [],
        10**9,
    )

    user += hop(send_user, "items", items, 0).astype(F32)
    rows = hot.shape[0] // 4
    high = lax.reduce_precision(hour, 8, 7)
    whole = high.astype(BF16)
    parts = [[hot[k * rows : (k + 1) * rows].astype(BF16), whole] for k in range(1, 4)]
    size = returned.shape[0] // 2
    parts[0].append(returned[size:].reshape(-1, rank_size))
    changes = (items, 2, items + 2)
    got = [
        turn(jnp.concatenate(part, axis=0), ("users", "items"), peers * items, change)
        for part, change in zip(parts, changes)
    ]
    back = got[0][rows + high_rows :]
    returned = jnp.concatenate([returned[:size], back.reshape(returned[:size].shape)], axis=1)
    got = [one[: rows + high_rows] for one in got]
    hot = hot[:rows] + sum(one[:rows].astype(F32) for one in got)
    by_user, by_item, by_both = [one[rows:].astype(F32) for one in got]
    hour = (high + by_item) + (by_user + by_both)

    last = bits_of(peers) - 1
    for bit in range(1, bits_of(peers)):
        rows, size = hot.shape[0] // 2, returned.shape[0] // 2
        high = lax.reduce_precision(hour, 8, 7)
        parts = [hot[rows:].astype(BF16), high.astype(BF16), returned[size:].reshape(-1, rank_size)]
        parts = jnp.concatenate(parts, axis=0)
        if bit == 1:
            parts, user, needs = lax.optimization_barrier((parts, user, needs))
        got = hop(parts, "users", peers, bit)
        if bit == 1:
            keep_user = user.shape[0] // 2
            got_user = hop(user[keep_user:].astype(BF16), "items", items, 1)
            needs = jnp.stack([needs, hop(needs, "users", peers, 0)], axis=1)
        if bit == last:
            user = user[:keep_user] + got_user.astype(F32)
            got, user, needs = lax.optimization_barrier((got, user, needs))
        back = got[rows + high_rows :]
        returned = jnp.concatenate([returned[:size], back.reshape(returned[:size].shape)], axis=1)
        hour = high + got[rows : rows + high_rows].astype(F32)
        if bit < last:
            hot = hot[:rows] + got[:rows].astype(F32)
    hot, got_hot = hot[:rows], got[:rows]
    mine = hour[:half]
    other = hop(mine, "items", items, 0)
    if not permute_hot:
        hot, got_hot = jnp.zeros((IB, rank_size), F32), jnp.zeros((IB, rank_size), BF16)
    cold_grad, hot = call(
        last_rows,
        (),
        (),
        (needs.reshape(-1, peers), returned.reshape(-1, rank_size), hot, got_hot),
        (shape(shard_len, rank_size), shape(hot.shape[0], rank_size)),
        [],
        10**8,
    )
    (hour_grad,) = call(last_hours, (), (), (mine, other), (shape(hours, rank_size),), [], 10**6)
    if not permute_hot:
        hot_whole = jnp.concatenate([hot_whole[part] for part in range(hot_whole.shape[0])], axis=1)
        hot = lax.psum_scatter(hot_whole, ("users", "items"), scatter_dimension=0, tiled=True)
    return (user, cold_grad, hot, hour_grad)


def solution(mesh):
    in_specs = (
        P("users", None),
        P(),
        P(("users", "items"), None),
        P(),
        P(("users", "items"), None),
        P(("users", "items"), None),
        P(("users", "items"), None),
        P(("users", "items")),
        P(("users", "items"), None, None),
        P(("users", "items"), None, None),
    )
    out_specs = (
        P(("users", "items"), None),
        P(("users", "items"), None),
        P(("users", "items"), None),
        P(),
    )
    return jax.shard_map(body, mesh=mesh, in_specs=in_specs, out_specs=out_specs, check_vma=False)
```

```python
import collections
import functools

import jax
import jax.numpy as jnp
from jax import lax
from jax.experimental import pallas as pl
from jax.experimental.pallas import tpu as pltpu
from jax.sharding import PartitionSpec as P

IB = 16
HB = 8
HALF = 128
F32 = jnp.float32
BF16 = jnp.bfloat16

Sizes = collections.namedtuple(
    "Sizes",
    ("peers", "items", "hot_slots", "reqs", "hours", "permute_hot", "split_hot", "hot_blocks", "cold_blocks"),
)


def bits_of(size):
    return size.bit_length() - 1


def padded(rows):
    return -(-rows // 16) * 16


def flip(value, bits):
    out = jnp.zeros_like(value)
    for k in range(bits):
        out = out | (((value >> k) & 1) << (bits - 1 - k))
    return out


def first_hours(hours):
    return (hours // HB + 1) // 2 * HB


def hour_of(lane, split, hours):
    half = first_hours(hours)
    side = (lane >= half).astype(jnp.int32)
    hour = (side ^ split) * half + lane - side * half
    return hour, (lane < 2 * half) & (hour < hours)


def one_hot(mask):
    return mask.astype(F32).astype(BF16)


def column(row):
    parts = [jnp.transpose(jnp.broadcast_to(row[:, k : k + 128], (128, 128))) for k in range(0, row.shape[1], 128)]
    return jnp.concatenate(parts, axis=0)


def spread(col, lanes):
    return jnp.concatenate([col] * (-(-lanes // 128)), axis=1)[:, :lanes]


def load_table(table, rows, at=0):
    for part in range(table.shape[0]):
        table[part, at : at + rows.shape[0], :] = rows[:, part * 128 : part * 128 + 128].astype(F32)


def chosen_blocks(sizes, hot, count, slot_row):
    place = lax.broadcasted_iota(jnp.int32, slot_row.shape, 1)
    of_kind = (slot_row < sizes.hot_slots) if hot else (slot_row >= sizes.hot_slots)
    chosen = (place < count) & of_kind
    return chosen, jnp.sum(chosen.astype(F32))


def prepare(sizes, hot, m, p, q, chosen, user, slot, hour, user_tab, observed, out, users_here=None):
    obs, live_hour, user_rows, pick, put, user_pos = out
    blocks = slot.shape[1]
    users = user_tab.shape[0]
    user_chunk = users // sizes.items

    kind = jnp.broadcast_to(chosen.astype(F32), (8, blocks)).astype(BF16)
    before = one_hot(
        lax.broadcasted_iota(jnp.int32, (blocks, blocks), 0) < lax.broadcasted_iota(jnp.int32, (blocks, blocks), 1)
    )
    rank = jnp.dot(kind, before, preferred_element_type=F32)[:1]
    rank = jnp.where(chosen, rank, -1.0).astype(jnp.int32)
    order = one_hot(rank == lax.broadcasted_iota(jnp.int32, (m, blocks), 0))
    user_in = user[...]
    rows = [user_in >> 4, user_in & 15, slot[...], hour[...] + 1]
    rows = jnp.concatenate([row.astype(F32) for row in rows] + [jnp.zeros((4, blocks), F32)], axis=0).astype(BF16)
    rows = lax.dot_general(rows, order, (((1,), (1,)), ((), ())), preferred_element_type=F32).astype(jnp.int32)
    user_row, slot_row, hour_row = rows[0:1] * 16 + rows[1:2], rows[2:3], rows[3:4] - 1
    obs[:m, :] = jnp.dot(order, 0.5 - observed[...], preferred_element_type=F32)

    user_col, hour_col = column(user_row), column(hour_row)
    if users_here is not None:
        users_here.wait()
    step = 512
    total = jnp.zeros((m, user_tab.shape[1]), F32)
    for k in range(0, users, step):
        lane = lax.broadcasted_iota(jnp.int32, (m, step), 1) + k
        total += jnp.dot(one_hot(spread(user_col, step) == lane), user_tab[k : k + step, :], preferred_element_type=F32)
    user_rows[:m, :] = total

    slots = pick.shape[1]
    if hot:
        put_pos = flip(slot_row ^ (p * sizes.items + q), bits_of(sizes.peers * sizes.items)) if sizes.permute_hot else slot_row
    else:
        owner, request = (slot_row - sizes.hot_slots) // sizes.reqs, (slot_row - sizes.hot_slots) % sizes.reqs
        put_pos = flip(owner ^ p, bits_of(sizes.peers)) * sizes.reqs + request
        slot_row = (owner ^ (p & ~1)) * sizes.reqs + request
    pick[:m, :] = one_hot(spread(column(slot_row), slots) == lax.broadcasted_iota(jnp.int32, (m, slots), 1))
    put[:, :m] = one_hot(put_pos == lax.broadcasted_iota(jnp.int32, (slots, m), 0))
    user_pos[:, :m] = flip((user_row // user_chunk) ^ q, bits_of(sizes.items)) * user_chunk + user_row % user_chunk

    lane = lax.broadcasted_iota(jnp.int32, (m, 2 * HALF), 1)
    lane_hour, used = hour_of(lane, q & 1, sizes.hours)
    live_hour[:m, :] = (used & ((lane_hour // HB) == spread(hour_col, 2 * HALF))).astype(F32)


def work(sizes, m, first, last, q, state, table, hours_tab, user_terms, item_sums, grad_hour, before=None, stack=8):
    obs, live_hour, user_rows, pick, put, _ = state
    slots = pick.shape[1]
    parts = range(table.shape[0])
    used = 2 * first_hours(sizes.hours)
    lane = lax.broadcasted_iota(jnp.int32, (IB * HB, 2 * HALF), 1)
    cell = lax.broadcasted_iota(jnp.int32, (IB * HB, 2 * HALF), 0)
    tile = one_hot(((cell & (HB - 1)) == (lane & (HB - 1))) & (((cell // HB) & 1) == lane // HALF))
    cell_pair = lax.broadcasted_iota(jnp.int32, (m, IB * HB), 1) // (2 * HB)

    def one(group, terms_before, hours_before):
        places = [group * stack + j for j in range(stack)]
        rows, cells = [], []
        for a in places:
            of_place = pl.ds(a, slots, stride=IB)
            choice = jnp.concatenate([table[part, of_place, :] for part in parts], axis=1).astype(BF16)
            rows.append(jnp.dot(pick[:m, :], choice, preferred_element_type=F32))
        for pair in range(stack // 2):
            cells.append(jnp.where(cell_pair == group * (stack // 2) + pair, obs[:m, :], 0.0).astype(BF16))
        users_f = user_rows[:m, :]
        user_item = jnp.concatenate([(users_f * row).astype(BF16) for row in rows], axis=0)
        half_model = lax.dot_general(
            user_item, hours_tab[...] * jnp.asarray(0.5, BF16), (((1,), (1,)), ((), ())), preferred_element_type=F32
        )
        pairs = jnp.dot(jnp.concatenate(cells, axis=0), tile, preferred_element_type=F32)
        seen = []
        for j in range(stack):
            one_place = pairs[j // 2 * m : j // 2 * m + m, j % 2 * HALF : j % 2 * HALF + HALF]
            seen.append(jnp.concatenate([one_place, one_place], axis=1))
        seen = jnp.concatenate(seen, axis=0)
        live = jnp.concatenate([live_hour[:m, :]] * stack, axis=0)
        residual = ((0.5 * jnp.tanh(half_model) + seen) * live).astype(BF16)
        weighted = jnp.dot(residual, hours_tab[...], preferred_element_type=F32)
        hour_terms = lax.dot_general(
            residual[:, :used], user_item, (((0,), (0,)), ((), ())), preferred_element_type=F32
        )
        grad_hour[...] = hour_terms + hours_before
        into = put[:, :m]
        total = terms_before
        for j, a in enumerate(places):
            mine = weighted[j * m : j * m + m]
            total += mine * rows[j]
            terms = mine * users_f
            high = terms.astype(BF16)
            low = (terms - high.astype(F32)).astype(BF16)
            sums = jnp.dot(into, high, preferred_element_type=F32) + jnp.dot(into, low, preferred_element_type=F32)
            for part in parts:
                item_sums[part, pl.ds(a, slots, stride=IB), :] = sums[:, part * 128 : part * 128 + 128]
        user_terms[:m, :] = total

    def next_one(group, carry):
        one(group, user_terms[:m, :], grad_hour[...])
        return carry

    if before is not None and last - first == stack:
        one(first // stack, *[0.0 if ref is None else ref[: size or ref.shape[0], :] for ref, size in zip(before, (m, None))])
    else:
        lax.fori_loop(first // stack, last // stack, next_one, 0)


def in_size(number, small, whole, run):
    small = small if isinstance(small, tuple) else (small,)
    pl.when(number <= small[0])(lambda: run(small[0]))
    for below, m in zip(small, small[1:]):
        pl.when((number > below) & (number <= m))(functools.partial(run, m))
    pl.when(number > small[-1])(lambda: run(whole))


def serve(sizes, *refs):
    turns = sizes.peers // 2
    needs, (mine, theirs), outs, table = refs[: -turns - 3], refs[-turns - 3 : -turns - 1], refs[-turns - 1 : -1], refs[-1]
    needs = [(need, k) for need in needs for k in range(need.shape[0])]
    p = lax.axis_index("users")
    rows = mine.shape[0]
    table[pl.ds(pl.multiple_of((p & 1) * rows, rows), rows), :] = mine[...]
    table[pl.ds(pl.multiple_of((1 - (p & 1)) * rows, rows), rows), :] = theirs[...]
    for m, out in enumerate(outs):
        for which in range(2):
            for r in range(sizes.reqs):
                owner = (p & ~1) + which
                block = needs[m][0][needs[m][1], r, owner]
                at = pl.multiple_of(which * rows + block * IB, IB)
                to = (which * sizes.reqs + r) * IB
                out[to : to + IB, :] = table[pl.ds(at, IB), :]


def start_copies(pairs, sems):
    copies = [pltpu.make_async_copy(source, target, sems.at[k]) for k, (source, target) in enumerate(pairs)]
    for copy in copies:
        copy.start()
    return copies


def first_kernel(
    sizes, count, user_in, slot_in, hour_in, user_tab_in, hot_in, hour_factor_in, observed_in,
    obs, live_hour, user_rows, pick, put, user_pos, table, hours_tab, user, slot, hour,
    user_tab, hot, hour_factor, observed, sems,
):
    state = (obs, live_hour, user_rows, pick, put, user_pos)
    p, q = lax.axis_index("users"), lax.axis_index("items")
    sources = (slot_in, user_in, hour_in, observed_in.at[0], hour_factor_in, hot_in, user_tab_in)
    copies = start_copies(zip(sources, (slot, user, hour, observed, hour_factor, hot, user_tab)), sems)
    for copy in copies[:3]:
        copy.wait()
    chosen, number = chosen_blocks(sizes, True, count[0], slot[...])
    for copy in copies[3:-1]:
        copy.wait()
    load_table(table, hot)
    row_hour, used = hour_of(lax.broadcasted_iota(jnp.int32, (2 * HALF, sizes.hours), 0), q & 1, sizes.hours)
    hit = one_hot(used & (row_hour == lax.broadcasted_iota(jnp.int32, (2 * HALF, sizes.hours), 1)))
    hours_tab[...] = jnp.dot(hit, hour_factor[...], preferred_element_type=F32).astype(BF16)

    def run(m):
        prepare(sizes, True, m, p, q, chosen, user, slot, hour, user_tab, observed, state, copies[-1])

    in_size(number, sizes.hot_blocks, slot.shape[1], run)


def half_kernel(
    sizes, count, obs, live_hour, user_rows, pick, put, user_pos, table, hours_tab, slot,
    user_terms, item_sums, grad_hour,
):
    state = (obs, live_hour, user_rows, pick, put, user_pos)
    q = lax.axis_index("items")
    _, number = chosen_blocks(sizes, True, count[0], slot[...])

    def run(m):
        before = (None, None)
        work(sizes, m, 0, IB // 2, q, state, table, hours_tab, user_terms, item_sums, grad_hour, before)

    in_size(number, (sizes.hot_blocks * 11 // 12, sizes.hot_blocks), slot.shape[1], run)


def second_kernel(
    sizes, count, user_tab_in, observed_in,
    obs, live_hour, user_rows, pick, put, user_pos, table, hours_tab, user, slot, hour,
    user_terms_in, item_sums_in, grad_hour_in,
    obs_2, live_hour_2, user_rows_2, pick_2, put_2, user_pos_2, user_terms, item_sums, grad_hour,
    user_tab, observed, sems,
):
    state = (obs, live_hour, user_rows, pick, put, user_pos)
    state_2 = (obs_2, live_hour_2, user_rows_2, pick_2, put_2, user_pos_2)
    p, q = lax.axis_index("users"), lax.axis_index("items")
    copies = start_copies(zip((observed_in.at[0], user_tab_in), (observed, user_tab)), sems)
    item_sums[...] = item_sums_in[...]
    _, number = chosen_blocks(sizes, True, count[0], slot[...])

    def run(m):
        before = (user_terms_in, grad_hour_in)
        work(sizes, m, IB // 2, IB, q, state, table, hours_tab, user_terms, item_sums, grad_hour, before)
        if m < user_terms.shape[0]:
            user_terms[m:, :] = jnp.zeros_like(user_terms[m:, :])

    in_size(number, (sizes.hot_blocks * 11 // 12, sizes.hot_blocks), slot.shape[1], run)
    chosen, number = chosen_blocks(sizes, False, count[0], slot[...])
    for copy in copies:
        copy.wait()

    def make(m):
        prepare(sizes, False, m, p, q, chosen, user, slot, hour, user_tab, observed, state_2)

    in_size(number, sizes.cold_blocks, slot.shape[1], make)


def third_kernel(
    sizes, count, slot, hours_tab,
    obs, live_hour, user_rows, pick, put, user_pos, hot_sums, grad_hour_in,
    *refs,
):
    fetched, (send, keep, cold_send, user_terms, table, item_sums, grad_hour) = refs[:-7], refs[-7:]
    state = (obs, live_hour, user_rows, pick, put, user_pos)
    q = lax.axis_index("items")
    rows = fetched[0].shape[0]
    for m, block in enumerate(fetched):
        load_table(table, block, m * rows)
    user_terms[...] = jnp.zeros_like(user_terms)
    grad_hour[...] = grad_hour_in[...]
    _, number = chosen_blocks(sizes, False, count[0], slot[...])

    def run(m):
        work(sizes, m, 0, IB, q, state, table, hours_tab, user_terms, item_sums, grad_hour)

    in_size(number, (sizes.cold_blocks // 4 * 3, sizes.cold_blocks), slot.shape[1], run)

    high_rows = padded(first_hours(sizes.hours))
    at = sizes.split_hot
    for part in range(table.shape[0]):
        lanes = slice(part * 128, part * 128 + 128)
        if at:
            keep[:at, lanes] = hot_sums[part, :at, :]
            send[:at, lanes] = hot_sums[part, at : 2 * at, :].astype(BF16)
        cold_send[:, lanes] = item_sums[part].astype(BF16)
    keep[at : at + high_rows, :] = grad_hour[:high_rows, :]
    half = first_hours(sizes.hours)
    other = jnp.concatenate([grad_hour[half:, :], jnp.zeros((high_rows - half, grad_hour.shape[1]), F32)], axis=0)
    high = other.astype(BF16)
    send[at : at + high_rows, :] = high
    send[at + high_rows : at + 2 * high_rows, :] = (other - high.astype(F32)).astype(BF16)


def users_kernel(sizes, count, slot, pos, terms, pos_2, terms_2, send, keep, step=256):
    _, number = chosen_blocks(sizes, True, count[0], slot[...])
    _, number_2 = chosen_blocks(sizes, False, count[0], slot[...])

    def add(m, m_2):
        total = jnp.concatenate([terms[:m, :], terms_2[:m_2, :]], axis=0)
        high = total.astype(BF16)
        low = (total - high.astype(F32)).astype(BF16)
        row = jnp.concatenate([pos[:, :m], pos_2[:, :m_2]], axis=1)
        within = one_hot((row & (step - 1)) == lax.broadcasted_iota(jnp.int32, (step, m + m_2), 0))
        for k in range(0, 2 * keep.shape[0], step):
            hit = within * one_hot((row // step) == k // step)
            sums = jnp.dot(hit, high, preferred_element_type=F32) + jnp.dot(hit, low, preferred_element_type=F32)
            if k < keep.shape[0]:
                keep[k : k + step, :] = sums
            else:
                send[k - keep.shape[0] : k - keep.shape[0] + step, :] = sums.astype(BF16)

    def hot(m):
        in_size(number_2, sizes.cold_blocks, slot.shape[1], lambda m_2: add(m, m_2))

    in_size(number, sizes.hot_blocks, slot.shape[1], hot)


def last_hours(sizes, mine, other, hour_grad):
    half = mine.shape[0]
    swap = (lax.axis_index("items") & 1) == 1
    rest = hour_grad.shape[0] - half
    hour_grad[:half, :] = jnp.where(swap, other[...], mine[...])
    hour_grad[half:, :] = jnp.where(swap, mine[:rest, :], other[:rest, :])


def last_rows(sizes, needs, returned, hot, got, cold_grad, hot_grad):
    p = lax.axis_index("users")
    hot_grad[...] = hot[...] + got[...].astype(F32)
    asked, rows = needs.shape[0], returned.shape[0]
    lane = lax.broadcasted_iota(jnp.int32, needs.shape, 1)
    mask = jnp.where(lane == p, needs[...], 0).astype(F32)
    wanted = jnp.broadcast_to(jnp.sum(mask, axis=1, keepdims=True), (asked, 128)).astype(BF16)
    number = lax.broadcasted_iota(jnp.int32, (asked, rows), 1) // IB
    place = one_hot(number == lax.broadcasted_iota(jnp.int32, (asked, rows), 0))
    block = lax.dot_general(wanted, place, (((0,), (0,)), ((), ())), preferred_element_type=F32)[:1].astype(jnp.int32)
    size = (cold_grad.shape[0], rows)
    row, column = lax.broadcasted_iota(jnp.int32, size, 0), lax.broadcasted_iota(jnp.int32, size, 1)
    hit = one_hot((row // IB == block) & (row % IB == column % IB))
    cold_grad[...] = jnp.dot(hit, returned[...], preferred_element_type=F32)


def hop(values, axis, size, bit):
    return lax.ppermute(values, axis, [(i, i ^ (1 << bit)) for i in range(size)])


def turn(values, axis, size, change):
    return lax.ppermute(values, axis, [(i, i ^ change) for i in range(size)])


def halves(values):
    rows = values.shape[0] // 2
    return values[:rows], values[rows:]


def body(
    user_factor,
    hot_factor,
    cold_factor,
    hour_factor,
    block_user,
    block_slot,
    block_hour,
    block_count,
    need_rows,
    observed,
):
    rank_size = user_factor.shape[1]
    hours = hour_factor.shape[0]
    hot_rows = hot_factor.shape[0]
    shard_len = cold_factor.shape[0]
    peers, items = lax.axis_size("users"), lax.axis_size("items")
    reqs = need_rows.shape[2]
    half = first_hours(hours)
    blocks = block_user.shape[1]
    users = user_factor.shape[0]
    hot_slots, cold_slots = hot_rows // IB, peers * reqs
    permute_hot = hot_rows == IB * peers * items
    high_rows = padded(half)
    split_hot = hot_rows // 2 if permute_hot else 0
    sizes = Sizes(
        peers, items, hot_slots, reqs, hours, permute_hot, split_hot, blocks // 4 * 3, blocks // 2
    )
    vmem = pl.BlockSpec(memory_space=pltpu.VMEM)
    smem = pl.BlockSpec(memory_space=pltpu.SMEM)
    hbm = pl.BlockSpec(memory_space=pltpu.HBM)

    def shape(*dims, dtype=F32):
        return jax.ShapeDtypeStruct(dims, dtype)

    def state_of(slots):
        return (
            shape(blocks, IB * HB),
            shape(blocks, 2 * HALF),
            shape(blocks, rank_size),
            shape(blocks, slots, dtype=BF16),
            shape(slots, blocks, dtype=BF16),
            shape(1, blocks, dtype=jnp.int32),
        )

    def table_of(slots):
        return (rank_size // 128, slots * IB, 128)

    def call(function, scalar, far, near, out_shape, scratch, flops):
        return pl.pallas_call(
            functools.partial(function, sizes),
            out_shape=out_shape,
            in_specs=[smem] * len(scalar) + [hbm] * len(far) + [vmem] * len(near),
            out_specs=(vmem,) * len(out_shape),
            scratch_shapes=scratch,
            compiler_params=pltpu.CompilerParams(vmem_limit_bytes=24 * 1024 * 1024),
            cost_estimate=pl.CostEstimate(flops=flops, bytes_accessed=4 << 20, transcendentals=0),
            name=function.__name__,
        )(*scalar, *[pltpu.with_memory_space_constraint(value, pltpu.HBM) for value in far], *near)

    turns = peers // 2
    theirs = hop(cold_factor, "users", peers, 0)
    need = jnp.transpose(need_rows, (0, 2, 1))
    needs = [need, hop(need, "users", peers, 1)]

    def room(*dims, dtype=F32):
        return pltpu.VMEM(dims, dtype)

    row = shape(1, blocks, dtype=jnp.int32)
    sums = (shape(*table_of(hot_slots)), shape(2 * half, rank_size))
    users_room = room(*user_factor.shape, dtype=BF16)
    observed_room = room(*observed.shape[1:], dtype=BF16)
    hot_state = call(
        first_kernel,
        (block_count,),
        (block_user, block_slot, block_hour, user_factor, hot_factor, hour_factor, observed),
        (),
        state_of(hot_slots) + (shape(*table_of(hot_slots)), shape(2 * HALF, rank_size, dtype=BF16), row, row, row),
        [
            users_room,
            room(*hot_factor.shape, dtype=BF16),
            room(*hour_factor.shape, dtype=BF16),
            observed_room,
            pltpu.SemaphoreType.DMA((7,)),
        ],
        10**8,
    )
    hours_tab, slot_row = hot_state[-4], hot_state[-2]
    needs, hot_state, theirs = lax.optimization_barrier((needs, hot_state, theirs))
    for bit in range(2, bits_of(peers)):
        needs.append(hop(jnp.concatenate(needs, axis=0), "users", peers, bit))
    terms = (shape(blocks, rank_size),) + sums
    hot_sums = call(half_kernel, (block_count,), (), (*hot_state[:8], slot_row), terms, [], 3 * 10**9)
    served = call(
        serve,
        needs,
        (),
        (cold_factor, theirs),
        (shape(2 * reqs * IB, rank_size, dtype=BF16),) * turns,
        [room(2 * shard_len, rank_size, dtype=BF16)],
        10**6,
    )
    hot_state, hot_sums, served = lax.optimization_barrier((hot_state, hot_sums, served))
    fetched = [served[0]] + [turn(served[m], "users", peers, 2 * m) for m in range(1, turns)]
    needs = jnp.concatenate(needs, axis=0)
    cold_state = call(
        second_kernel,
        (block_count,),
        (user_factor, observed),
        (*hot_state, *hot_sums),
        state_of(cold_slots) + terms,
        [users_room, observed_room, pltpu.SemaphoreType.DMA((2,))],
        5 * 10**9,
    )
    *cold_state, hot_terms, hot_whole, hour_whole = cold_state
    send, keep, returned, cold_terms = call(
        third_kernel,
        (block_count,),
        (),
        (slot_row, hours_tab, *cold_state, hot_whole, hour_whole, *fetched),
        (
            shape(split_hot + 2 * high_rows, rank_size, dtype=BF16),
            shape(split_hot + high_rows, rank_size),
            shape(cold_slots * IB, rank_size, dtype=BF16),
            shape(blocks, rank_size),
        ),
        [room(*table_of(cold_slots)), room(*table_of(cold_slots)), room(2 * half, rank_size)],
        5 * 10**9,
    )
    returned = returned.reshape(peers, reqs * IB, rank_size)
    got = hop(send, "items", items, 0)
    got, cold_terms = lax.optimization_barrier((got, cold_terms))
    hot = keep[:split_hot] + got[:split_hot].astype(F32)
    hour = keep[split_hot:] + got[split_hot : split_hot + high_rows].astype(F32)
    hour += got[split_hot + high_rows :].astype(F32)
    send_user, user = call(
        users_kernel,
        (block_count,),
        (),
        (slot_row, hot_state[5], hot_terms, cold_state[5], cold_terms),
        (shape(users // 2, rank_size, dtype=BF16), shape(users // 2, rank_size)),
        [],
        10**9,
    )

    user += hop(send_user, "items", items, 0).astype(F32)
    rows = hot.shape[0] // 4
    high = lax.reduce_precision(hour, 8, 7)
    whole = high.astype(BF16)
    parts = [[hot[k * rows : (k + 1) * rows].astype(BF16), whole] for k in range(1, 4)]
    size = returned.shape[0] // 2
    parts[0].append(returned[size:].reshape(-1, rank_size))
    changes = (items, 2, items + 2)
    got = [
        turn(jnp.concatenate(part, axis=0), ("users", "items"), peers * items, change)
        for part, change in zip(parts, changes)
    ]
    back = got[0][rows + high_rows :]
    returned = jnp.concatenate([returned[:size], back.reshape(returned[:size].shape)], axis=1)
    got = [one[: rows + high_rows] for one in got]
    hot = hot[:rows] + sum(one[:rows].astype(F32) for one in got)
    by_user, by_item, by_both = [one[rows:].astype(F32) for one in got]
    hour = (high + by_item) + (by_user + by_both)

    last = bits_of(peers) - 1
    for bit in range(1, bits_of(peers)):
        rows, size = hot.shape[0] // 2, returned.shape[0] // 2
        high = lax.reduce_precision(hour, 8, 7)
        parts = [hot[rows:].astype(BF16), high.astype(BF16), returned[size:].reshape(-1, rank_size)]
        parts = jnp.concatenate(parts, axis=0)
        if bit == 1:
            parts, user, needs = lax.optimization_barrier((parts, user, needs))
        got = hop(parts, "users", peers, bit)
        if bit == 1:
            keep_user = user.shape[0] // 2
            got_user = hop(user[keep_user:].astype(BF16), "items", items, 1)
            needs = jnp.stack([needs, hop(needs, "users", peers, 0)], axis=1)
        if bit == last:
            user = user[:keep_user] + got_user.astype(F32)
            got, user, needs = lax.optimization_barrier((got, user, needs))
        back = got[rows + high_rows :]
        returned = jnp.concatenate([returned[:size], back.reshape(returned[:size].shape)], axis=1)
        hour = high + got[rows : rows + high_rows].astype(F32)
        if bit < last:
            hot = hot[:rows] + got[:rows].astype(F32)
    hot, got_hot = hot[:rows], got[:rows]
    mine = hour[:half]
    other = hop(mine, "items", items, 0)
    if not permute_hot:
        hot, got_hot = jnp.zeros((IB, rank_size), F32), jnp.zeros((IB, rank_size), BF16)
    cold_grad, hot = call(
        last_rows,
        (),
        (),
        (needs.reshape(-1, peers), returned.reshape(-1, rank_size), hot, got_hot),
        (shape(shard_len, rank_size), shape(hot.shape[0], rank_size)),
        [],
        10**8,
    )
    (hour_grad,) = call(last_hours, (), (), (mine, other), (shape(hours, rank_size),), [], 10**6)
    if not permute_hot:
        hot_whole = jnp.concatenate([hot_whole[part] for part in range(hot_whole.shape[0])], axis=1)
        hot = lax.psum_scatter(hot_whole, ("users", "items"), scatter_dimension=0, tiled=True)
    return (user, cold_grad, hot, hour_grad)


def solution(mesh):
    in_specs = (
        P("users", None),
        P(),
        P(("users", "items"), None),
        P(),
        P(("users", "items"), None),
        P(("users", "items"), None),
        P(("users", "items"), None),
        P(("users", "items")),
        P(("users", "items"), None, None),
        P(("users", "items"), None, None),
    )
    out_specs = (
        P(("users", "items"), None),
        P(("users", "items"), None),
        P(("users", "items"), None),
        P(),
    )
    return jax.shard_map(body, mesh=mesh, in_specs=in_specs, out_specs=out_specs, check_vma=False)
```

```python
import collections
import functools

import jax
import jax.numpy as jnp
from jax import lax
from jax.experimental import pallas as pl
from jax.experimental.pallas import tpu as pltpu
from jax.sharding import PartitionSpec as P

IB = 16
HB = 8
HALF = 128
F32 = jnp.float32
BF16 = jnp.bfloat16

Sizes = collections.namedtuple(
    "Sizes",
    ("peers", "items", "hot_slots", "reqs", "hours", "permute_hot", "split_hot", "hot_blocks", "cold_blocks"),
)


def bits_of(size):
    return size.bit_length() - 1


def padded(rows):
    return -(-rows // 16) * 16


def flip(value, bits):
    out = jnp.zeros_like(value)
    for k in range(bits):
        out = out | (((value >> k) & 1) << (bits - 1 - k))
    return out


def first_hours(hours):
    return (hours // HB + 1) // 2 * HB


def hour_of(lane, split, hours):
    half = first_hours(hours)
    side = (lane >= half).astype(jnp.int32)
    hour = (side ^ split) * half + lane - side * half
    return hour, (lane < 2 * half) & (hour < hours)


def one_hot(mask):
    return mask.astype(F32).astype(BF16)


def column(row):
    parts = [jnp.transpose(jnp.broadcast_to(row[:, k : k + 128], (128, 128))) for k in range(0, row.shape[1], 128)]
    return jnp.concatenate(parts, axis=0)


def spread(col, lanes):
    return jnp.concatenate([col] * (-(-lanes // 128)), axis=1)[:, :lanes]


def load_table(table, rows, at=0):
    for part in range(table.shape[0]):
        table[part, at : at + rows.shape[0], :] = rows[:, part * 128 : part * 128 + 128].astype(F32)


def chosen_blocks(sizes, hot, count, slot_row):
    place = lax.broadcasted_iota(jnp.int32, slot_row.shape, 1)
    of_kind = (slot_row < sizes.hot_slots) if hot else (slot_row >= sizes.hot_slots)
    chosen = (place < count) & of_kind
    return chosen, jnp.sum(chosen.astype(F32))


def prepare(sizes, hot, m, p, q, chosen, user, slot, hour, user_tab, observed, out, users_here=None):
    obs, live_hour, user_rows, pick, put, user_pos = out
    blocks = slot.shape[1]
    users = user_tab.shape[0]
    user_chunk = users // sizes.items

    kind = jnp.broadcast_to(chosen.astype(F32), (8, blocks)).astype(BF16)
    before = one_hot(
        lax.broadcasted_iota(jnp.int32, (blocks, blocks), 0) < lax.broadcasted_iota(jnp.int32, (blocks, blocks), 1)
    )
    rank = jnp.dot(kind, before, preferred_element_type=F32)[:1]
    rank = jnp.where(chosen, rank, -1.0).astype(jnp.int32)
    order = one_hot(rank == lax.broadcasted_iota(jnp.int32, (m, blocks), 0))
    user_in = user[...]
    rows = [user_in >> 4, user_in & 15, slot[...], hour[...] + 1]
    rows = jnp.concatenate([row.astype(F32) for row in rows] + [jnp.zeros((4, blocks), F32)], axis=0).astype(BF16)
    rows = lax.dot_general(rows, order, (((1,), (1,)), ((), ())), preferred_element_type=F32).astype(jnp.int32)
    user_row, slot_row, hour_row = rows[0:1] * 16 + rows[1:2], rows[2:3], rows[3:4] - 1
    obs[:m, :] = jnp.dot(order, 0.5 - observed[...], preferred_element_type=F32)

    user_col, hour_col = column(user_row), column(hour_row)
    if users_here is not None:
        users_here.wait()
    step = 512
    total = jnp.zeros((m, user_tab.shape[1]), F32)
    for k in range(0, users, step):
        lane = lax.broadcasted_iota(jnp.int32, (m, step), 1) + k
        total += jnp.dot(one_hot(spread(user_col, step) == lane), user_tab[k : k + step, :], preferred_element_type=F32)
    user_rows[:m, :] = total

    slots = pick.shape[1]
    if hot:
        put_pos = flip(slot_row ^ (p * sizes.items + q), bits_of(sizes.peers * sizes.items)) if sizes.permute_hot else slot_row
    else:
        owner, request = (slot_row - sizes.hot_slots) // sizes.reqs, (slot_row - sizes.hot_slots) % sizes.reqs
        put_pos = flip(owner ^ p, bits_of(sizes.peers)) * sizes.reqs + request
        slot_row = (owner ^ (p & ~1)) * sizes.reqs + request
    pick[:m, :] = one_hot(spread(column(slot_row), slots) == lax.broadcasted_iota(jnp.int32, (m, slots), 1))
    put[:, :m] = one_hot(put_pos == lax.broadcasted_iota(jnp.int32, (slots, m), 0))
    user_pos[:, :m] = flip((user_row // user_chunk) ^ q, bits_of(sizes.items)) * user_chunk + user_row % user_chunk

    lane = lax.broadcasted_iota(jnp.int32, (m, 2 * HALF), 1)
    lane_hour, used = hour_of(lane, q & 1, sizes.hours)
    live_hour[:m, :] = (used & ((lane_hour // HB) == spread(hour_col, 2 * HALF))).astype(F32)


def work(sizes, m, first, last, q, state, table, hours_tab, user_terms, item_sums, grad_hour, before=None, stack=8, fine=True):
    obs, live_hour, user_rows, pick, put, _ = state
    slots = pick.shape[1]
    parts = range(table.shape[0])
    used = 2 * first_hours(sizes.hours)
    lane = lax.broadcasted_iota(jnp.int32, (IB * HB, 2 * HALF), 1)
    cell = lax.broadcasted_iota(jnp.int32, (IB * HB, 2 * HALF), 0)
    tile = one_hot(((cell & (HB - 1)) == (lane & (HB - 1))) & (((cell // HB) & 1) == lane // HALF))
    cell_pair = lax.broadcasted_iota(jnp.int32, (m, IB * HB), 1) // (2 * HB)

    def one(group, terms_before, hours_before):
        places = [group * stack + j for j in range(stack)]
        rows, cells = [], []
        for a in places:
            of_place = pl.ds(a, slots, stride=IB)
            choice = jnp.concatenate([table[part, of_place, :] for part in parts], axis=1).astype(BF16)
            rows.append(jnp.dot(pick[:m, :], choice, preferred_element_type=F32))
        for pair in range(stack // 2):
            cells.append(jnp.where(cell_pair == group * (stack // 2) + pair, obs[:m, :], 0.0).astype(BF16))
        users_f = user_rows[:m, :]
        user_item = jnp.concatenate([(users_f * row).astype(BF16) for row in rows], axis=0)
        half_model = lax.dot_general(
            user_item, hours_tab[...] * jnp.asarray(0.5, BF16), (((1,), (1,)), ((), ())), preferred_element_type=F32
        )
        pairs = jnp.dot(jnp.concatenate(cells, axis=0), tile, preferred_element_type=F32)
        seen = []
        for j in range(stack):
            one_place = pairs[j // 2 * m : j // 2 * m + m, j % 2 * HALF : j % 2 * HALF + HALF]
            seen.append(jnp.concatenate([one_place, one_place], axis=1))
        seen = jnp.concatenate(seen, axis=0)
        live = jnp.concatenate([live_hour[:m, :]] * stack, axis=0)
        residual = ((0.5 * jnp.tanh(half_model) + seen) * live).astype(BF16)
        weighted = jnp.dot(residual, hours_tab[...], preferred_element_type=F32)
        hour_terms = lax.dot_general(
            residual[:, :used], user_item, (((0,), (0,)), ((), ())), preferred_element_type=F32
        )
        grad_hour[...] = hour_terms + hours_before
        into = put[:, :m]
        total = terms_before
        for j, a in enumerate(places):
            mine = weighted[j * m : j * m + m]
            total += mine * rows[j]
            terms = mine * users_f
            high = terms.astype(BF16)
            sums = jnp.dot(into, high, preferred_element_type=F32)
            if fine:
                low = (terms - high.astype(F32)).astype(BF16)
                sums += jnp.dot(into, low, preferred_element_type=F32)
            for part in parts:
                item_sums[part, pl.ds(a, slots, stride=IB), :] = sums[:, part * 128 : part * 128 + 128]
        user_terms[:m, :] = total

    def next_one(group, carry):
        one(group, user_terms[:m, :], grad_hour[...])
        return carry

    if before is not None and last - first == stack:
        one(first // stack, *[0.0 if ref is None else ref[: size or ref.shape[0], :] for ref, size in zip(before, (m, None))])
    else:
        lax.fori_loop(first // stack, last // stack, next_one, 0)


def in_size(number, small, whole, run):
    small = small if isinstance(small, tuple) else (small,)
    pl.when(number <= small[0])(lambda: run(small[0]))
    for below, m in zip(small, small[1:]):
        pl.when((number > below) & (number <= m))(functools.partial(run, m))
    pl.when(number > small[-1])(lambda: run(whole))


def serve(sizes, *refs):
    turns = sizes.peers // 2
    needs, (mine, theirs), outs, table = refs[: -turns - 3], refs[-turns - 3 : -turns - 1], refs[-turns - 1 : -1], refs[-1]
    needs = [(need, k) for need in needs for k in range(need.shape[0])]
    p = lax.axis_index("users")
    rows = mine.shape[0]
    table[pl.ds(pl.multiple_of((p & 1) * rows, rows), rows), :] = mine[...]
    table[pl.ds(pl.multiple_of((1 - (p & 1)) * rows, rows), rows), :] = theirs[...]
    for m, out in enumerate(outs):
        for which in range(2):
            for r in range(sizes.reqs):
                owner = (p & ~1) + which
                block = needs[m][0][needs[m][1], r, owner]
                at = pl.multiple_of(which * rows + block * IB, IB)
                to = (which * sizes.reqs + r) * IB
                out[to : to + IB, :] = table[pl.ds(at, IB), :]


def start_copies(pairs, sems):
    copies = [pltpu.make_async_copy(source, target, sems.at[k]) for k, (source, target) in enumerate(pairs)]
    for copy in copies:
        copy.start()
    return copies


def first_kernel(
    sizes, count, user_in, slot_in, hour_in, user_tab_in, hot_in, hour_factor_in, observed_in,
    obs, live_hour, user_rows, pick, put, user_pos, table, hours_tab, user, slot, hour,
    user_tab, hot, hour_factor, observed, sems,
):
    state = (obs, live_hour, user_rows, pick, put, user_pos)
    p, q = lax.axis_index("users"), lax.axis_index("items")
    sources = (slot_in, user_in, hour_in, observed_in.at[0], hour_factor_in, hot_in, user_tab_in)
    copies = start_copies(zip(sources, (slot, user, hour, observed, hour_factor, hot, user_tab)), sems)
    for copy in copies[:3]:
        copy.wait()
    chosen, number = chosen_blocks(sizes, True, count[0], slot[...])
    for copy in copies[3:-1]:
        copy.wait()
    load_table(table, hot)
    row_hour, used = hour_of(lax.broadcasted_iota(jnp.int32, (2 * HALF, sizes.hours), 0), q & 1, sizes.hours)
    hit = one_hot(used & (row_hour == lax.broadcasted_iota(jnp.int32, (2 * HALF, sizes.hours), 1)))
    hours_tab[...] = jnp.dot(hit, hour_factor[...], preferred_element_type=F32).astype(BF16)

    def run(m):
        prepare(sizes, True, m, p, q, chosen, user, slot, hour, user_tab, observed, state, copies[-1])

    in_size(number, sizes.hot_blocks, slot.shape[1], run)


def half_kernel(
    sizes, count, obs, live_hour, user_rows, pick, put, user_pos, table, hours_tab, slot,
    user_terms, item_sums, grad_hour,
):
    state = (obs, live_hour, user_rows, pick, put, user_pos)
    q = lax.axis_index("items")
    _, number = chosen_blocks(sizes, True, count[0], slot[...])

    def run(m):
        before = (None, None)
        work(sizes, m, 0, IB // 2, q, state, table, hours_tab, user_terms, item_sums, grad_hour, before)

    in_size(number, (sizes.hot_blocks * 11 // 12, sizes.hot_blocks), slot.shape[1], run)


def second_kernel(
    sizes, count, user_tab_in, observed_in,
    obs, live_hour, user_rows, pick, put, user_pos, table, hours_tab, user, slot, hour,
    user_terms_in, item_sums_in, grad_hour_in,
    obs_2, live_hour_2, user_rows_2, pick_2, put_2, user_pos_2, user_terms, item_sums, grad_hour,
    user_tab, observed, sems,
):
    state = (obs, live_hour, user_rows, pick, put, user_pos)
    state_2 = (obs_2, live_hour_2, user_rows_2, pick_2, put_2, user_pos_2)
    p, q = lax.axis_index("users"), lax.axis_index("items")
    copies = start_copies(zip((observed_in.at[0], user_tab_in), (observed, user_tab)), sems)
    item_sums[...] = item_sums_in[...]
    _, number = chosen_blocks(sizes, True, count[0], slot[...])

    def run(m):
        before = (user_terms_in, grad_hour_in)
        work(sizes, m, IB // 2, IB, q, state, table, hours_tab, user_terms, item_sums, grad_hour, before)
        if m < user_terms.shape[0]:
            user_terms[m:, :] = jnp.zeros_like(user_terms[m:, :])

    in_size(number, (sizes.hot_blocks * 11 // 12, sizes.hot_blocks), slot.shape[1], run)
    chosen, number = chosen_blocks(sizes, False, count[0], slot[...])
    for copy in copies:
        copy.wait()

    def make(m):
        prepare(sizes, False, m, p, q, chosen, user, slot, hour, user_tab, observed, state_2)

    in_size(number, sizes.cold_blocks, slot.shape[1], make)


def third_kernel(
    sizes, count, slot, hours_tab,
    obs, live_hour, user_rows, pick, put, user_pos, hot_sums, grad_hour_in,
    *refs,
):
    fetched, (send, keep, cold_send, user_terms, table, item_sums, grad_hour) = refs[:-7], refs[-7:]
    state = (obs, live_hour, user_rows, pick, put, user_pos)
    q = lax.axis_index("items")
    rows = fetched[0].shape[0]
    for m, block in enumerate(fetched):
        load_table(table, block, m * rows)
    user_terms[...] = jnp.zeros_like(user_terms)
    grad_hour[...] = grad_hour_in[...]
    _, number = chosen_blocks(sizes, False, count[0], slot[...])

    def run(m):
        work(sizes, m, 0, IB, q, state, table, hours_tab, user_terms, item_sums, grad_hour, fine=False)

    in_size(number, (sizes.cold_blocks // 4 * 3, sizes.cold_blocks), slot.shape[1], run)

    high_rows = padded(first_hours(sizes.hours))
    at = sizes.split_hot
    for part in range(table.shape[0]):
        lanes = slice(part * 128, part * 128 + 128)
        if at:
            keep[:at, lanes] = hot_sums[part, :at, :]
            send[:at, lanes] = hot_sums[part, at : 2 * at, :].astype(BF16)
        cold_send[:, lanes] = item_sums[part].astype(BF16)
    keep[at : at + high_rows, :] = grad_hour[:high_rows, :]
    half = first_hours(sizes.hours)
    other = jnp.concatenate([grad_hour[half:, :], jnp.zeros((high_rows - half, grad_hour.shape[1]), F32)], axis=0)
    high = other.astype(BF16)
    send[at : at + high_rows, :] = high
    send[at + high_rows : at + 2 * high_rows, :] = (other - high.astype(F32)).astype(BF16)


def users_kernel(sizes, count, slot, pos, terms, pos_2, terms_2, send, keep, step=256):
    _, number = chosen_blocks(sizes, True, count[0], slot[...])
    _, number_2 = chosen_blocks(sizes, False, count[0], slot[...])

    def add(m, m_2):
        total = jnp.concatenate([terms[:m, :], terms_2[:m_2, :]], axis=0)
        high = total.astype(BF16)
        low = (total - high.astype(F32)).astype(BF16)
        row = jnp.concatenate([pos[:, :m], pos_2[:, :m_2]], axis=1)
        within = one_hot((row & (step - 1)) == lax.broadcasted_iota(jnp.int32, (step, m + m_2), 0))
        for k in range(0, 2 * keep.shape[0], step):
            hit = within * one_hot((row // step) == k // step)
            sums = jnp.dot(hit, high, preferred_element_type=F32) + jnp.dot(hit, low, preferred_element_type=F32)
            if k < keep.shape[0]:
                keep[k : k + step, :] = sums
            else:
                send[k - keep.shape[0] : k - keep.shape[0] + step, :] = sums.astype(BF16)

    def hot(m):
        in_size(number_2, sizes.cold_blocks, slot.shape[1], lambda m_2: add(m, m_2))

    in_size(number, sizes.hot_blocks, slot.shape[1], hot)


def last_hours(sizes, mine, other, hour_grad):
    half = mine.shape[0]
    swap = (lax.axis_index("items") & 1) == 1
    rest = hour_grad.shape[0] - half
    hour_grad[:half, :] = jnp.where(swap, other[...], mine[...])
    hour_grad[half:, :] = jnp.where(swap, mine[:rest, :], other[:rest, :])


def last_rows(sizes, needs, returned, hot, got, cold_grad, hot_grad):
    p = lax.axis_index("users")
    hot_grad[...] = hot[...] + got[...].astype(F32)
    asked, rows = needs.shape[0], returned.shape[0]
    lane = lax.broadcasted_iota(jnp.int32, needs.shape, 1)
    mask = jnp.where(lane == p, needs[...], 0).astype(F32)
    wanted = jnp.broadcast_to(jnp.sum(mask, axis=1, keepdims=True), (asked, 128)).astype(BF16)
    number = lax.broadcasted_iota(jnp.int32, (asked, rows), 1) // IB
    place = one_hot(number == lax.broadcasted_iota(jnp.int32, (asked, rows), 0))
    block = lax.dot_general(wanted, place, (((0,), (0,)), ((), ())), preferred_element_type=F32)[:1].astype(jnp.int32)
    size = (cold_grad.shape[0], rows)
    row, column = lax.broadcasted_iota(jnp.int32, size, 0), lax.broadcasted_iota(jnp.int32, size, 1)
    hit = one_hot((row // IB == block) & (row % IB == column % IB))
    cold_grad[...] = jnp.dot(hit, returned[...], preferred_element_type=F32)


def hop(values, axis, size, bit):
    return lax.ppermute(values, axis, [(i, i ^ (1 << bit)) for i in range(size)])


def turn(values, axis, size, change):
    return lax.ppermute(values, axis, [(i, i ^ change) for i in range(size)])


def halves(values):
    rows = values.shape[0] // 2
    return values[:rows], values[rows:]


def body(
    user_factor,
    hot_factor,
    cold_factor,
    hour_factor,
    block_user,
    block_slot,
    block_hour,
    block_count,
    need_rows,
    observed,
):
    rank_size = user_factor.shape[1]
    hours = hour_factor.shape[0]
    hot_rows = hot_factor.shape[0]
    shard_len = cold_factor.shape[0]
    peers, items = lax.axis_size("users"), lax.axis_size("items")
    reqs = need_rows.shape[2]
    half = first_hours(hours)
    blocks = block_user.shape[1]
    users = user_factor.shape[0]
    hot_slots, cold_slots = hot_rows // IB, peers * reqs
    permute_hot = hot_rows == IB * peers * items
    high_rows = padded(half)
    split_hot = hot_rows // 2 if permute_hot else 0
    sizes = Sizes(
        peers, items, hot_slots, reqs, hours, permute_hot, split_hot, blocks // 4 * 3, blocks // 2
    )
    vmem = pl.BlockSpec(memory_space=pltpu.VMEM)
    smem = pl.BlockSpec(memory_space=pltpu.SMEM)
    hbm = pl.BlockSpec(memory_space=pltpu.HBM)

    def shape(*dims, dtype=F32):
        return jax.ShapeDtypeStruct(dims, dtype)

    def state_of(slots):
        return (
            shape(blocks, IB * HB),
            shape(blocks, 2 * HALF),
            shape(blocks, rank_size),
            shape(blocks, slots, dtype=BF16),
            shape(slots, blocks, dtype=BF16),
            shape(1, blocks, dtype=jnp.int32),
        )

    def table_of(slots):
        return (rank_size // 128, slots * IB, 128)

    def call(function, scalar, far, near, out_shape, scratch, flops):
        return pl.pallas_call(
            functools.partial(function, sizes),
            out_shape=out_shape,
            in_specs=[smem] * len(scalar) + [hbm] * len(far) + [vmem] * len(near),
            out_specs=(vmem,) * len(out_shape),
            scratch_shapes=scratch,
            compiler_params=pltpu.CompilerParams(vmem_limit_bytes=24 * 1024 * 1024),
            cost_estimate=pl.CostEstimate(flops=flops, bytes_accessed=4 << 20, transcendentals=0),
            name=function.__name__,
        )(*scalar, *[pltpu.with_memory_space_constraint(value, pltpu.HBM) for value in far], *near)

    turns = peers // 2
    theirs = hop(cold_factor, "users", peers, 0)
    need = jnp.transpose(need_rows, (0, 2, 1))
    needs = [need, hop(need, "users", peers, 1)]

    def room(*dims, dtype=F32):
        return pltpu.VMEM(dims, dtype)

    row = shape(1, blocks, dtype=jnp.int32)
    sums = (shape(*table_of(hot_slots)), shape(2 * half, rank_size))
    users_room = room(*user_factor.shape, dtype=BF16)
    observed_room = room(*observed.shape[1:], dtype=BF16)
    hot_state = call(
        first_kernel,
        (block_count,),
        (block_user, block_slot, block_hour, user_factor, hot_factor, hour_factor, observed),
        (),
        state_of(hot_slots) + (shape(*table_of(hot_slots)), shape(2 * HALF, rank_size, dtype=BF16), row, row, row),
        [
            users_room,
            room(*hot_factor.shape, dtype=BF16),
            room(*hour_factor.shape, dtype=BF16),
            observed_room,
            pltpu.SemaphoreType.DMA((7,)),
        ],
        10**8,
    )
    hours_tab, slot_row = hot_state[-4], hot_state[-2]
    needs, hot_state, theirs = lax.optimization_barrier((needs, hot_state, theirs))
    for bit in range(2, bits_of(peers)):
        needs.append(hop(jnp.concatenate(needs, axis=0), "users", peers, bit))
    terms = (shape(blocks, rank_size),) + sums
    hot_sums = call(half_kernel, (block_count,), (), (*hot_state[:8], slot_row), terms, [], 3 * 10**9)
    served = call(
        serve,
        needs,
        (),
        (cold_factor, theirs),
        (shape(2 * reqs * IB, rank_size, dtype=BF16),) * turns,
        [room(2 * shard_len, rank_size, dtype=BF16)],
        10**6,
    )
    hot_state, hot_sums, served = lax.optimization_barrier((hot_state, hot_sums, served))
    fetched = [served[0]] + [turn(served[m], "users", peers, 2 * m) for m in range(1, turns)]
    needs = jnp.concatenate(needs, axis=0)
    cold_state = call(
        second_kernel,
        (block_count,),
        (user_factor, observed),
        (*hot_state, *hot_sums),
        state_of(cold_slots) + terms,
        [users_room, observed_room, pltpu.SemaphoreType.DMA((2,))],
        5 * 10**9,
    )
    *cold_state, hot_terms, hot_whole, hour_whole = cold_state
    send, keep, returned, cold_terms = call(
        third_kernel,
        (block_count,),
        (),
        (slot_row, hours_tab, *cold_state, hot_whole, hour_whole, *fetched),
        (
            shape(split_hot + 2 * high_rows, rank_size, dtype=BF16),
            shape(split_hot + high_rows, rank_size),
            shape(cold_slots * IB, rank_size, dtype=BF16),
            shape(blocks, rank_size),
        ),
        [room(*table_of(cold_slots)), room(*table_of(cold_slots)), room(2 * half, rank_size)],
        5 * 10**9,
    )
    returned = returned.reshape(peers, reqs * IB, rank_size)
    got = hop(send, "items", items, 0)
    got, cold_terms = lax.optimization_barrier((got, cold_terms))
    hot = keep[:split_hot] + got[:split_hot].astype(F32)
    hour = keep[split_hot:] + got[split_hot : split_hot + high_rows].astype(F32)
    hour = (hour + got[split_hot + high_rows :].astype(F32))[:half]
    send_user, user = call(
        users_kernel,
        (block_count,),
        (),
        (slot_row, hot_state[5], hot_terms, cold_state[5], cold_terms),
        (shape(users // 2, rank_size, dtype=BF16), shape(users // 2, rank_size)),
        [],
        10**9,
    )

    user += hop(send_user, "items", items, 0).astype(F32)
    rows = hot.shape[0] // 4
    high = lax.reduce_precision(hour, 8, 7)
    whole = high.astype(BF16)
    parts = [[hot[k * rows : (k + 1) * rows].astype(BF16), whole] for k in range(1, 4)]
    size = returned.shape[0] // 2
    parts[0].append(returned[size:].reshape(-1, rank_size))
    changes = (items, 2, items + 2)
    got = [
        turn(jnp.concatenate(part, axis=0), ("users", "items"), peers * items, change)
        for part, change in zip(parts, changes)
    ]
    back = got[0][rows + half :]
    returned = jnp.concatenate([returned[:size], back.reshape(returned[:size].shape)], axis=1)
    got = [one[: rows + half] for one in got]
    hot = hot[:rows] + sum(one[:rows].astype(F32) for one in got)
    by_user, by_item, by_both = [one[rows:].astype(F32) for one in got]
    hour = (high + by_item) + (by_user + by_both)

    last = bits_of(peers) - 1
    for bit in range(1, bits_of(peers)):
        rows, size = hot.shape[0] // 2, returned.shape[0] // 2
        high = lax.reduce_precision(hour, 8, 7)
        parts = [hot[rows:].astype(BF16), high.astype(BF16), returned[size:].reshape(-1, rank_size)]
        parts = jnp.concatenate(parts, axis=0)
        if bit == 1:
            parts, user, needs = lax.optimization_barrier((parts, user, needs))
        got = hop(parts, "users", peers, bit)
        if bit == 1:
            keep_user = user.shape[0] // 2
            got_user = hop(user[keep_user:].astype(BF16), "items", items, 1)
            needs = jnp.stack([needs, hop(needs, "users", peers, 0)], axis=1)
        if bit == last:
            user = user[:keep_user] + got_user.astype(F32)
            got, user, needs = lax.optimization_barrier((got, user, needs))
        back = got[rows + half :]
        returned = jnp.concatenate([returned[:size], back.reshape(returned[:size].shape)], axis=1)
        hour = high + got[rows : rows + half].astype(F32)
        if bit < last:
            hot = hot[:rows] + got[:rows].astype(F32)
    hot, got_hot = hot[:rows], got[:rows]
    mine = hour[:half]
    other = hop(mine, "items", items, 0)
    if not permute_hot:
        hot, got_hot = jnp.zeros((IB, rank_size), F32), jnp.zeros((IB, rank_size), BF16)
    cold_grad, hot = call(
        last_rows,
        (),
        (),
        (needs.reshape(-1, peers), returned.reshape(-1, rank_size), hot, got_hot),
        (shape(shard_len, rank_size), shape(hot.shape[0], rank_size)),
        [],
        10**8,
    )
    (hour_grad,) = call(last_hours, (), (), (mine, other), (shape(hours, rank_size),), [], 10**6)
    if not permute_hot:
        hot_whole = jnp.concatenate([hot_whole[part] for part in range(hot_whole.shape[0])], axis=1)
        hot = lax.psum_scatter(hot_whole, ("users", "items"), scatter_dimension=0, tiled=True)
    return (user, cold_grad, hot, hour_grad)


def solution(mesh):
    in_specs = (
        P("users", None),
        P(),
        P(("users", "items"), None),
        P(),
        P(("users", "items"), None),
        P(("users", "items"), None),
        P(("users", "items"), None),
        P(("users", "items")),
        P(("users", "items"), None, None),
        P(("users", "items"), None, None),
    )
    out_specs = (
        P(("users", "items"), None),
        P(("users", "items"), None),
        P(("users", "items"), None),
        P(),
    )
    return jax.shard_map(body, mesh=mesh, in_specs=in_specs, out_specs=out_specs, check_vma=False)
```
